256 devices in a mesh: horiz: 64 (over x, z, core), depth: 4 (over y).
Axes of the slice: x: 4, y: 4, z: 8, core: 2. Of those that a mesh axis runs over, the one named last changes fastest.
Arguments:
- initial_state: float32 [4, 256, 8, 128], P(None, 'horiz', 'depth'), may hold values from 0 to 2
- explicit_blocks: float32 [256, 8, 4, 128, 128], P('horiz', 'depth'), may hold values from -0.0625 to 0.0625
- implicit_blocks: float32 [256, 8, 4, 128, 128], P('horiz', 'depth'), may hold values from -0.0625 to 0.0625
- pattern: int32 [256, 8, 4], P('horiz', 'depth'), may hold values from 0 to 24, as said below
- cavity_mask: int32 [256, 8, 128], P('horiz', 'depth'), may hold values 0 or 1
- melt_rate: float32 [256, 8, 128], P('horiz', 'depth'), may hold values from 0.2 to 2
- uptake_rate: float32 [256, 8, 128], P('horiz', 'depth'), may hold values from 0.2 to 2
Outputs:
- spun_up: float32 [4, 256, 8, 128], P(None, 'horiz', 'depth')
The draws below stay inside these ranges and needn't reach their ends.
Inputs may be any that keep to these rules, and one draw needn't show every extreme that they name: `pattern`: code 5 (a + 2) + (b + 2) names the block a positions away horizontally and b in depth; the 4 codes of one block row differ.
All inputs are finite; a program needn't handle non-finite values. No bound on the sum of `cavity_mask` on one device may be relied on, other than what follows from the above.
Results may differ from the reference program's by a relative error of at most 0.0015.
Values sent between devices are 32-bit elements; how exact they have to be, the bound alone decides.
A program may use at most 64 MiB of HBM per device.

```python
import math
import jax
import jax.numpy as jnp
from jax import lax

BLOCK = 128
TRACERS = 4
KBLOCKS = 4
NEWTON = 2
KRYLOV = 3
NBH = 256
NBD = 8


def draw_pattern(key, part):
    key = jax.random.fold_in(key, 7)
    scores = jax.random.randint(key, (NBH, NBD, 25), 0, 1 << 20) * 32 + jnp.arange(25, dtype=jnp.int32)
    ordered = jnp.argsort(scores, axis=-1)
    return ordered[..., :KBLOCKS].astype(jnp.int32)


def set_ends(result, key, least, largest):
    spot = [jax.random.randint(jax.random.fold_in(key, axis), (), 0, length) for axis, length in enumerate(result.shape)]
    widest = result.shape.index(max(result.shape))
    neighbour = spot[:widest] + [(spot[widest] + 1) % result.shape[widest]] + spot[widest + 1:]
    return result.at[tuple(spot)].set(least).at[tuple(neighbour)].set(largest)


def block_levels(key, dims, split, low, largest):
    level = 1.0
    for position, parts in split:
        heights = jax.random.uniform(jax.random.fold_in(jax.random.fold_in(key, 6), position), (parts,), jnp.float32, low / len(split), largest / len(split))
        level = level * jnp.repeat(jnp.exp(heights), dims[position] // parts).reshape((-1,) + (1,) * (len(dims) - 1 - position))
    return level


def normal_values(rng, dims, width, most, cuts=(), kind=jnp.bfloat16):
    gain = block_levels(rng, dims, cuts, -0.22, 0.18) if cuts else 1.0
    result = jax.random.normal(rng, dims, jnp.float32) * width * gain
    return jnp.minimum(jnp.maximum(result, -most), most).astype(kind)


def setup_inputs(seed: int = 0) -> dict:
    key_of = jax.random.split(jax.random.key(seed), 8)
    return {
        "initial_state": jnp.clip(2.0 * jax.random.uniform(key_of[0], (TRACERS, NBH, NBD, BLOCK), jnp.float32) ** block_levels(key_of[0], (TRACERS, NBH, NBD, BLOCK), ((1, 64), (2, 4)), -0.2, 0.2), 0.0, 2.0),
        "explicit_blocks": normal_values(key_of[1], (NBH, NBD, KBLOCKS, BLOCK, BLOCK), (16 * KBLOCKS * BLOCK) ** -0.5, 0.0625, ((0, 64), (1, 4)), jnp.float32),
        "implicit_blocks": normal_values(key_of[2], (NBH, NBD, KBLOCKS, BLOCK, BLOCK), (16 * KBLOCKS * BLOCK) ** -0.5, 0.0625, ((0, 64), (1, 4)), jnp.float32),
        "pattern": draw_pattern(jax.random.fold_in(key_of[7], 71), 0),
        "cavity_mask": set_ends((jax.random.randint(key_of[4], (NBH, NBD, BLOCK), 0, 2) < 1).astype(jnp.int32), jax.random.fold_in(key_of[4], 1), 0, 1),
        "melt_rate": jnp.clip(jnp.exp(math.log(2.0) - 2.3025851 * jax.random.uniform(key_of[5], (NBH, NBD, BLOCK), jnp.float32) ** block_levels(key_of[5], (NBH, NBD, BLOCK), ((0, 64), (1, 4)), -0.2, 0.2)), 0.2, 2.0),
        "uptake_rate": jnp.clip(jnp.exp(math.log(2.0) - 2.3025851 * jax.random.uniform(key_of[6], (NBH, NBD, BLOCK), jnp.float32) ** block_levels(key_of[6], (NBH, NBD, BLOCK), ((0, 64), (1, 4)), -0.2, 0.2)), 0.2, 2.0),
    }


time_step = 0.5
highest = lax.Precision.HIGHEST

def one_hot_codes(pattern):
    return (pattern[..., None] == jnp.arange(25, dtype=jnp.int32)).astype(jnp.float32)

def block_product(padded, blocks, offset_codes):
    extent_horiz = offset_codes.shape[0]
    extent_depth = offset_codes.shape[1]
    shifted_views = [padded[:, offset // 5:offset // 5 + extent_horiz, offset % 5:offset % 5 + extent_depth, :] for offset in range(25)]
    stacked = jnp.stack(shifted_views)
    chosen = jnp.einsum('hdkc,cthdj->thdkj', offset_codes, stacked, precision=highest)
    return jnp.einsum('hdkij,thdkj->thdi', blocks, chosen, precision=highest)

def sources(tracers, forcing, uptake):
    iron_level = tracers[3]
    squared = iron_level * iron_level
    limitation = squared / (1.0 + squared)
    uptake_flux = uptake * tracers[1] * limitation
    return jnp.stack([forcing * (1.0 - tracers[0]), -uptake_flux, 0.5 * uptake_flux - 0.2 * tracers[2], forcing * tracers[0] - 0.05 * uptake_flux])

def source_tangent(tracers, direction, forcing, uptake):
    iron_level = tracers[3]
    denominator = 1.0 + iron_level * iron_level
    limitation = iron_level * iron_level / denominator
    slope_term = 2.0 * iron_level / (denominator * denominator)
    flux_change = uptake * (direction[1] * limitation + tracers[1] * slope_term * direction[3])
    return jnp.stack([-forcing * direction[0], -flux_change, 0.5 * flux_change - 0.2 * direction[2], forcing * direction[0] - 0.05 * flux_change])

def least_squares(hessenberg, start_norm):
    columns_count = hessenberg.shape[1]
    rotated = hessenberg
    target = jnp.zeros((columns_count + 1,), jnp.float32).at[0].set(start_norm)
    for column in range(columns_count):
        pivot_top = rotated[column, column]
        second = rotated[column + 1, column]
        radius = jnp.sqrt(pivot_top * pivot_top + second * second)
        cosine = pivot_top / radius
        sine_value = second / radius
        row_top = rotated[column]
        row_low = rotated[column + 1]
        rotated = rotated.at[column].set(cosine * row_top + sine_value * row_low).at[column + 1].set(cosine * row_low - sine_value * row_top)
        target_top = target[column]
        target_low = target[column + 1]
        target = target.at[column].set(cosine * target_top + sine_value * target_low).at[column + 1].set(cosine * target_low - sine_value * target_top)
    solution = jnp.zeros((columns_count,), jnp.float32)
    for column in reversed(range(columns_count)):
        partial_sum = target[column] - jnp.sum(rotated[column, column + 1:] * solution[column + 1:])
        solution = solution.at[column].set(partial_sum / rotated[column, column])
    return solution

def reference(initial_state, explicit_blocks, implicit_blocks, pattern, cavity_mask, melt_rate, uptake_rate):
    offset_codes = one_hot_codes(pattern)
    forcing = cavity_mask.astype(jnp.float32) * melt_rate

    def ghosts(tracer_field):
        return jnp.pad(tracer_field, ((0, 0), (2, 2), (2, 2), (0, 0)))

    def transport(tracer_field, source_term):
        middle = 0.5 * tracer_field + block_product(ghosts(tracer_field), explicit_blocks, offset_codes) + time_step * source_term
        return middle + block_product(ghosts(middle), implicit_blocks, offset_codes)
    current = initial_state
    for newton_step in range(NEWTON):
        residual = current - transport(current, sources(current, forcing, uptake_rate))
        start_norm = jnp.sqrt(jnp.sum(residual * residual))
        basis = [residual / start_norm]
        hessenberg = jnp.zeros((KRYLOV + 1, KRYLOV), jnp.float32)
        for column in range(KRYLOV):
            vector = basis[column]
            mapped = transport(vector, source_tangent(current, vector, forcing, uptake_rate)) - vector
            stacked = jnp.stack(basis)
            products = jnp.einsum('ntabc,tabc->n', stacked, mapped, precision=highest)
            mapped = mapped - jnp.einsum('n,ntabc->tabc', products, stacked, precision=highest)
            norm_value = jnp.sqrt(jnp.sum(mapped * mapped))
            hessenberg = hessenberg.at[:column + 1, column].set(products).at[column + 1, column].set(norm_value)
            if column + 1 < KRYLOV:
                basis.append(mapped / norm_value)
        weights = least_squares(hessenberg, start_norm)
        current = current + jnp.einsum('n,ntabc->tabc', weights, jnp.stack(basis), precision=highest)
    return current
```

```python
import functools
import jax
import jax.numpy as jnp
from jax import lax
from jax.experimental import pallas as pl
from jax.experimental.pallas import tpu as pltpu
from jax.sharding import PartitionSpec as P

NEWTON = 2
KRYLOV = 3
SHIFT = 0.4

f32 = jnp.float32
bf16 = jnp.bfloat16
MESH = pl.DeviceIdType.MESH

SLOT = 192
OWN = 80
UPTAKE = 15
SLOTS = 16
ZERO = SLOTS * SLOT

DIRECTIONS = [(sh, sd) for sd in (-1, 0, 1) for sh in (-1, 0, 1) if (sh, sd) != (0, 0)]


def rows(start, size):
    return pl.ds(pl.multiple_of(start, 16) if not isinstance(start, int) else start, size)


def kernel(
    nh, nd, ga, c_in, a_hbm, b_hbm, pat, mask, melt, upt, out,
    X, GB, IDX, st_a, st_b, WA, WB, PR, FU, K, RA, RB,
    w_sem, r_sem, s_sem, ra_sem, rb_sem, rs_sem,
):
    gb = (nh // ga) * nd
    h = lax.axis_index("horiz")
    d = lax.axis_index("depth")

    copy_a = pltpu.make_async_copy(a_hbm, st_a, w_sem.at[0])
    copy_b = pltpu.make_async_copy(b_hbm, st_b, w_sem.at[1])
    copy_a.start()
    copy_b.start()

    h_hi = h // ga
    h_lo = lax.rem(h, ga)
    index_b = h_hi * nd + d

    def neighbour(sh, sd):
        return (lax.rem(h + sh + nh, nh), lax.rem(d + sd + nd, nd))

    def partner_a(k):
        return (h_hi * ga + lax.rem(h_lo + k, ga), d)

    def partner_b(k):
        index = lax.rem(index_b + k, gb)
        return ((index // nd) * ga + h_lo, lax.rem(index, nd))

    barrier = pltpu.get_barrier_semaphore()
    for sh, sd in DIRECTIONS:
        pl.semaphore_signal(barrier, inc=1, device_id=neighbour(sh, sd), device_id_type=MESH)

    def greet_a(k, _):
        pl.semaphore_signal(barrier, inc=1, device_id=partner_a(k), device_id_type=MESH)
        return 0

    def greet_b(k, _):
        pl.semaphore_signal(barrier, inc=1, device_id=partner_b(k), device_id_type=MESH)
        return 0

    lax.fori_loop(1, ga, greet_a, 0)
    lax.fori_loop(1, gb, greet_b, 0)

    for hh in range(4):
        for dd in range(2):
            o = hh * 2 + dd
            for t in range(4):
                X[pl.ds(OWN + o * 4 + t, 1), :] = c_in[t, hh, pl.ds(dd, 1), :]
            u_row = upt[hh, pl.ds(dd, 1), :]
            X[pl.ds(UPTAKE * SLOT + OWN + o * 4, 4), :] = jnp.broadcast_to(u_row, (4, 128))
            FU[pl.ds(o, 1), :] = mask[hh, pl.ds(dd, 1), :].astype(f32) * melt[hh, pl.ds(dd, 1), :]
            FU[pl.ds(8 + o, 1), :] = u_row
    X[pl.ds(ZERO, 32), :] = jnp.zeros((32, 128), f32)

    for o in range(8):
        for k in range(4):
            code = pat[o // 2, o % 2, k]
            five = lax.div(code, 5)
            row = (o // 2) + five
            dep = (o % 2) + code - 5 * five
            band = lax.div(dep, 2)
            IDX[o * 4 + k] = band * 16 + row * 2 + dep - 2 * band

    pl.semaphore_wait(barrier, 8 + (ga - 1) + (gb - 1))

    starts = []
    for sh, sd in DIRECTIONS:
        n_rows = 16 if sh else 32
        src_h = {1: 4, -1: 2, 0: 2}[sh]
        dst_h = {1: 0, -1: 6, 0: 2}[sh]
        inside = jnp.logical_and(
            jnp.logical_and(h + sh >= 0, h + sh < nh), jnp.logical_and(d + sd >= 0, d + sd < nd)
        )
        starts.append(
            (inside, (16 + src_h * 2) * 4, ((1 - sd) * 16 + dst_h * 2) * 4, n_rows, neighbour(sh, sd))
        )

    def exchange(slot):
        base = slot * SLOT
        for inside, src, dst, n_rows, target in starts:
            pltpu.make_async_remote_copy(
                src_ref=X.at[rows(jnp.where(inside, base + src, ZERO), n_rows)],
                dst_ref=X.at[rows(base + dst, n_rows)],
                send_sem=s_sem.at[slot],
                recv_sem=r_sem.at[slot],
                device_id=target,
                device_id_type=MESH,
            ).start()

    def arrived(slot, sem):
        span = X.at[rows(slot * SLOT, SLOT - 32)]
        pltpu.make_async_copy(span, span, sem.at[slot]).wait()

    def own(slot):
        return [X[pl.ds(slot * SLOT + OWN + t, 8, stride=4), :] for t in range(4)]

    def set_own(slot, value):
        for t in range(4):
            X[pl.ds(slot * SLOT + OWN + t, 8, stride=4), :] = value[t]

    def split_blocks(stage, weights):
        def body(o, _):
            for k in range(4):
                block = stage[o // 2, lax.rem(o, 2), k]
                high = block.astype(bf16)
                weights[o, pl.ds(0, 128), pl.ds(k * 128, 128)] = high
                weights[o, pl.ds(128, 128), pl.ds(k * 128, 128)] = (block - high.astype(f32)).astype(bf16)
            return 0

        lax.fori_loop(0, 8, body, 0)

    upper = lax.broadcasted_iota(jnp.int32, (8, 128), 0) < 4

    def product(slot, weights):
        for pair in range(24):
            x = X[pl.ds(pl.multiple_of(slot * SLOT + pair * 8, 8), 8), :]
            high = x.astype(bf16).astype(f32)
            low = pltpu.roll(x - high, 4, axis=0)
            GB[2 * pair] = jnp.where(upper, high, low)
            GB[2 * pair + 1] = jnp.where(upper, low, high)
        for pair in range(4):
            sums = []
            for o in (2 * pair, 2 * pair + 1):
                lhs = jnp.concatenate(
                    [
                        GB[IDX[o * 4 + k]].astype(bf16)
                        for k in range(4)
                    ],
                    axis=1,
                )
                both = lax.dot_general(
                    lhs, weights[o], (((1,), (1,)), ((), ())), preferred_element_type=f32
                )
                both = both[:, :128] + both[:, 128:]
                sums.append(both + pltpu.roll(both, 4, axis=0))
            PR[pl.ds(pair * 8, 8), :] = jnp.where(upper, sums[0], sums[1])
        return [PR[pl.ds(t, 8, stride=4), :] for t in range(4)]

    def all_sum(step, row):
        RA[step, h_lo] = row

        def send_a(k, _):
            pltpu.make_async_remote_copy(
                src_ref=RA.at[step, h_lo], dst_ref=RA.at[step, h_lo],
                send_sem=rs_sem.at[2 * step], recv_sem=ra_sem.at[step],
                device_id=partner_a(k), device_id_type=MESH,
            ).start()
            return 0

        lax.fori_loop(1, ga, send_a, 0)
        span = RA.at[step, pl.ds(0, ga - 1)]
        pltpu.make_async_copy(span, span, ra_sem.at[step]).wait()
        RB[step, index_b] = jnp.sum(RA[step], axis=0)

        def send_b(k, _):
            pltpu.make_async_remote_copy(
                src_ref=RB.at[step, index_b], dst_ref=RB.at[step, index_b],
                send_sem=rs_sem.at[2 * step + 1], recv_sem=rb_sem.at[step],
                device_id=partner_b(k), device_id_type=MESH,
            ).start()
            return 0

        lax.fori_loop(1, gb, send_b, 0)
        span = RB.at[step, pl.ds(0, gb - 1)]
        pltpu.make_async_copy(span, span, rb_sem.at[step]).wait()
        return jnp.sum(RB[step], axis=0)

    lane = lax.broadcasted_iota(jnp.int32, (1, 128), 1)

    def coefficients(step):
        vectors = [[K[j * 4 + t] for t in range(4)] for j in range(4)]
        pairs = [(i, j) for i in range(4) for j in range(i, 4)]
        row = jnp.zeros((1, 128), f32)
        for number, (i, j) in enumerate(pairs):
            part = sum(vectors[i][t] * vectors[j][t] for t in range(4))
            total = jnp.sum(jnp.sum(part, axis=0, keepdims=True), axis=1, keepdims=True)
            row = jnp.where(lane == number, total, row)
        total = all_sum(step, row)
        gram = {
            pair: jnp.sum(jnp.where(lane == number, total, 0.0), axis=1, keepdims=True)
            for number, pair in enumerate(pairs)
        }
        zero = jnp.zeros((1, 1), f32)
        R = [[zero] * 4 for _ in range(4)]
        for i in range(4):
            pivot = gram[i, i]
            for m in range(i):
                pivot = pivot - R[m][i] * R[m][i]
            pivot = jnp.maximum(pivot, 1e-14 * gram[i, i])
            R[i][i] = jnp.sqrt(pivot)
            inverse = 1.0 / R[i][i]
            for j in range(i + 1, 4):
                value = gram[i, j]
                for m in range(i):
                    value = value - R[m][i] * R[m][j]
                R[i][j] = value * inverse
        hess = [[(SHIFT - 1.0) * R[i][j] + R[i][j + 1] for j in range(3)] for i in range(4)]
        target = [R[0][0], zero, zero, zero]
        for c in range(3):
            top, low = hess[c][c], hess[c + 1][c]
            inverse = 1.0 / jnp.sqrt(top * top + low * low)
            cosine, sine = top * inverse, low * inverse
            for j in range(c, 3):
                top, low = hess[c][j], hess[c + 1][j]
                hess[c][j] = cosine * top + sine * low
                hess[c + 1][j] = cosine * low - sine * top
            top, low = target[c], target[c + 1]
            target[c] = cosine * top + sine * low
            target[c + 1] = cosine * low - sine * top
        answer = [zero] * 3
        for c in (2, 1, 0):
            value = target[c]
            for j in range(c + 1, 3):
                value = value - hess[c][j] * answer[j]
            answer[c] = value / hess[c][c]
        return answer

    def limitation(iron):
        squared = iron * iron
        return squared / (1.0 + squared)

    def slope(iron):
        denominator = 1.0 + iron * iron
        return 2.0 * iron / (denominator * denominator)

    def krylov(first, c, residual):
        forcing, uptake = FU[pl.ds(0, 8), :], FU[pl.ds(8, 8), :]
        flux_one = uptake * limitation(c[3])
        flux_three = uptake * c[1] * slope(c[3])
        for t in range(4):
            K[t] = residual[t]

        def step(j, _):
            v = [K[4 * j + t] for t in range(4)]
            slot = first + 2 * j
            set_own(slot, v)
            exchange(slot)
            change = flux_one * v[1] + flux_three * v[3]
            middle = [
                0.5 * v[0] - 0.5 * forcing * v[0],
                0.5 * v[1] - 0.5 * change,
                0.4 * v[2] + 0.25 * change,
                0.5 * v[3] + 0.5 * forcing * v[0] - 0.025 * change,
            ]
            arrived(slot, r_sem)
            image = product(slot, WA)
            middle = [m + i for m, i in zip(middle, image)]
            set_own(slot + 1, middle)
            exchange(slot + 1)
            arrived(slot + 1, r_sem)
            image = product(slot + 1, WB)
            for t in range(4):
                K[4 * (j + 1) + t] = middle[t] + image[t] - SHIFT * v[t]
            return 0

        lax.fori_loop(0, KRYLOV, step, 0)

    exchange(0)
    exchange(UPTAKE)
    copy_a.wait()
    split_blocks(st_a, WA)
    arrived(0, r_sem)
    image = product(0, WA)
    c = own(0)
    forcing, uptake = FU[pl.ds(0, 8), :], FU[pl.ds(8, 8), :]
    flux = uptake * c[1] * limitation(c[3])
    source = [
        forcing * (1.0 - c[0]),
        -flux,
        0.5 * flux - 0.2 * c[2],
        forcing * c[0] - 0.05 * flux,
    ]
    middle = [0.5 * c[t] + image[t] + 0.5 * source[t] for t in range(4)]
    set_own(1, middle)
    exchange(1)
    copy_b.wait()
    split_blocks(st_b, WB)
    arrived(1, r_sem)
    image = product(1, WB)
    krylov(2, c, [c[t] - middle[t] - image[t] for t in range(4)])
    weights = coefficients(0)

    arrived(UPTAKE, r_sem)

    def wide(slot, t):
        return X[pl.ds(slot * SLOT + t, 48, stride=4), :]

    def wide_sum(first_slot, t):
        return sum(weights[j] * wide(first_slot + 2 * j, t) for j in range(3))

    tracer_old, iron_old = wide(0, 1), wide(0, 3)
    iron_step = wide_sum(2, 3)
    tracer_new, iron_new = tracer_old + wide_sum(2, 1), iron_old + iron_step
    rest = wide(UPTAKE, 0) * (
        tracer_new * (limitation(iron_new) - limitation(iron_old)) - tracer_old * slope(iron_old) * iron_step
    )
    for t in range(4):
        value = wide(1, t) + wide_sum(3, t)
        if t:
            value = value + (0.0, -0.5, 0.25, -0.025)[t] * rest
        X[pl.ds(8 * SLOT + t, 48, stride=4), :] = value
    image = product(8, WB)
    middle = own(8)
    c = [own(0)[t] + sum(weights[j] * K[4 * j + t] for j in range(3)) for t in range(4)]

    krylov(9, c, [c[t] - middle[t] - image[t] for t in range(4)])
    weights = coefficients(1)
    for t in range(4):
        out[pl.ds(t, 8, stride=4), :] = c[t] + sum(weights[j] * K[4 * j + t] for j in range(3))

    for slot in (0, 1, 2, 3, 4, 5, 6, 7, 9, 10, 11, 12, 13, 14, UPTAKE):
        arrived(slot, s_sem)
    for step in range(NEWTON):
        span = RA.at[step, pl.ds(0, ga - 1)]
        pltpu.make_async_copy(span, span, rs_sem.at[2 * step]).wait()
        span = RB.at[step, pl.ds(0, gb - 1)]
        pltpu.make_async_copy(span, span, rs_sem.at[2 * step + 1]).wait()


def per_device(nh, nd, state, explicit_blocks, implicit_blocks, pattern, cavity_mask, melt_rate, uptake_rate):
    ga = 16 if nh % 16 == 0 else 2
    gb = (nh // ga) * nd
    vmem = pl.BlockSpec(memory_space=pltpu.VMEM)
    result = pl.pallas_call(
        functools.partial(kernel, nh, nd, ga),
        out_shape=jax.ShapeDtypeStruct((32, 128), f32),
        in_specs=[
            vmem,
            pl.BlockSpec(memory_space=pl.ANY),
            pl.BlockSpec(memory_space=pl.ANY),
            pl.BlockSpec(memory_space=pltpu.SMEM),
            vmem,
            vmem,
            vmem,
        ],
        out_specs=vmem,
        scratch_shapes=[
            pltpu.VMEM((SLOTS * SLOT + 32, 128), f32),
            pltpu.VMEM((48, 8, 128), f32),
            pltpu.SMEM((32,), jnp.int32),
            pltpu.VMEM((4, 2, 4, 128, 128), f32),
            pltpu.VMEM((4, 2, 4, 128, 128), f32),
            pltpu.VMEM((8, 256, 512), bf16),
            pltpu.VMEM((8, 256, 512), bf16),
            pltpu.VMEM((32, 128), f32),
            pltpu.VMEM((16, 128), f32),
            pltpu.VMEM((16, 8, 128), f32),
            pltpu.VMEM((NEWTON, ga, 1, 128), f32),
            pltpu.VMEM((NEWTON, gb, 1, 128), f32),
            pltpu.SemaphoreType.DMA((2,)),
            pltpu.SemaphoreType.DMA((SLOTS,)),
            pltpu.SemaphoreType.DMA((SLOTS,)),
            pltpu.SemaphoreType.DMA((NEWTON,)),
            pltpu.SemaphoreType.DMA((NEWTON,)),
            pltpu.SemaphoreType.DMA((2 * NEWTON,)),
        ],
        compiler_params=pltpu.CompilerParams(
            collective_id=0, has_side_effects=True, vmem_limit_bytes=24 * 1024 * 1024
        ),
    )(state, explicit_blocks, implicit_blocks, pattern, cavity_mask, melt_rate, uptake_rate)
    return result.reshape(4, 2, 4, 128).transpose(2, 0, 1, 3)


def solution(mesh):
    nh, nd = mesh.shape["horiz"], mesh.shape["depth"]
    return jax.shard_map(
        functools.partial(per_device, nh, nd),
        mesh=mesh,
        in_specs=(
            P(None, "horiz", "depth", None),
            P("horiz", "depth", None, None, None),
            P("horiz", "depth", None, None, None),
            P("horiz", "depth", None),
            P("horiz", "depth", None),
            P("horiz", "depth", None),
            P("horiz", "depth", None),
        ),
        out_specs=P(None, "horiz", "depth", None),
        check_vma=False,
    )
```

```python
import functools
import jax
import jax.numpy as jnp
from jax import lax
from jax.experimental import pallas as pl
from jax.experimental.pallas import tpu as pltpu
from jax.sharding import PartitionSpec as P

NEWTON = 2
KRYLOV = 3
SHIFT = 0.3

f32 = jnp.float32
bf16 = jnp.bfloat16
MESH = pl.DeviceIdType.MESH

SLOT = 192
OWN = 80
UPTAKE = 15
SLOTS = 16
ZERO = SLOTS * SLOT

DIRECTIONS = [(1, 1), (-1, 1), (1, -1), (-1, -1), (0, 1), (0, -1), (1, 0), (-1, 0)]


def rows(start, size):
    return pl.ds(pl.multiple_of(start, 16) if not isinstance(start, int) else start, size)


def kernel(
    nh, nd, ga, c_hbm, a_hbm, b_hbm, pat_hbm, mask_hbm, melt_hbm, upt_hbm, out,
    c_in, pat, mask, melt, upt, X, GB, IDX, st_a, st_b, WA, WB, PR, FU, K, RA, RB,
    w_sem, r_sem, s_sem, ra_sem, rb_sem, rs_sem,
):
    gb = (nh // ga) * nd
    h = lax.axis_index("horiz")
    d = lax.axis_index("depth")

    small = [
        pltpu.make_async_copy(source, target, w_sem.at[2 + number])
        for number, (source, target) in enumerate(
            [(c_hbm, c_in), (upt_hbm, upt), (pat_hbm, pat), (mask_hbm, mask), (melt_hbm, melt)]
        )
    ]
    for copy in small:
        copy.start()
    copy_a = pltpu.make_async_copy(a_hbm, st_a, w_sem.at[0])
    copy_b = pltpu.make_async_copy(b_hbm, st_b, w_sem.at[1])
    copy_a.start()
    copy_b.start()

    h_hi = h // ga
    h_lo = lax.rem(h, ga)
    index_b = h_hi * nd + d

    sends = []
    for sh, sd in DIRECTIONS:
        n_rows = 16 if sh else 32
        src_h = {1: 4, -1: 2, 0: 2}[sh]
        dst_h = {1: 0, -1: 6, 0: 2}[sh]
        in_h = jnp.logical_and(h + sh >= 0, h + sh < nh)
        in_d = jnp.logical_and(d + sd >= 0, d + sd < nd)
        other_d = d + 1 - 2 * lax.rem(d, 2)
        other_h = h + 1 - 2 * lax.rem(h, 2)
        near_h = h + sh if sh else other_h
        target = (
            jnp.where(in_h, jnp.where(in_d, h + sh, near_h), h),
            jnp.where(in_h, jnp.where(in_d, d + sd, d), other_d),
        )
        far_h = {1: 6, -1: 0, 0: 2}[sh]
        position = jnp.where(
            in_h,
            jnp.where(in_d, (1 - sd) * 16 + dst_h * 2, (1 + sd) * 16 + dst_h * 2),
            (1 - sd) * 16 + far_h * 2,
        )
        sends.append((jnp.logical_and(in_h, in_d), (16 + src_h * 2) * 4, position * 4, n_rows, target))

    def partner_a(k):
        return (h_hi * ga + lax.rem(h_lo + k, ga), d)

    def partner_b(k):
        index = lax.rem(index_b + k, gb)
        return ((index // nd) * ga + h_lo, lax.rem(index, nd))

    barrier = pltpu.get_barrier_semaphore()
    for *_, target in sends:
        pl.semaphore_signal(barrier, inc=1, device_id=target, device_id_type=MESH)

    def greet_a(k, _):
        pl.semaphore_signal(barrier, inc=1, device_id=partner_a(k), device_id_type=MESH)
        return 0

    def greet_b(k, _):
        pl.semaphore_signal(barrier, inc=1, device_id=partner_b(k), device_id_type=MESH)
        return 0

    lax.fori_loop(1, ga, greet_a, 0)
    lax.fori_loop(1, gb, greet_b, 0)

    for copy in small:
        copy.wait()
    for hh in range(4):
        for dd in range(2):
            o = hh * 2 + dd
            for t in range(4):
                X[pl.ds(OWN + o * 4 + t, 1), :] = c_in[t, hh, pl.ds(dd, 1), :]
            u_row = upt[hh, pl.ds(dd, 1), :]
            X[pl.ds(UPTAKE * SLOT + OWN + o * 4, 4), :] = jnp.broadcast_to(u_row, (4, 128))
            FU[pl.ds(o, 1), :] = mask[hh, pl.ds(dd, 1), :].astype(f32) * melt[hh, pl.ds(dd, 1), :]
            FU[pl.ds(8 + o, 1), :] = u_row
    X[pl.ds(ZERO, 32), :] = jnp.zeros((32, 128), f32)

    for o in range(8):
        for k in range(4):
            code = pat[o // 2, o % 2, k]
            five = lax.div(code, 5)
            row = (o // 2) + five
            dep = (o % 2) + code - 5 * five
            band = lax.div(dep, 2)
            IDX[o * 4 + k] = band * 16 + row * 2 + dep - 2 * band

    pl.semaphore_wait(barrier, 8 + (ga - 1) + (gb - 1))

    def exchange(slot):
        base = slot * SLOT
        for inside, src, dst, n_rows, target in sends:
            pltpu.make_async_remote_copy(
                src_ref=X.at[rows(jnp.where(inside, base + src, ZERO), n_rows)],
                dst_ref=X.at[rows(base + dst, n_rows)],
                send_sem=s_sem.at[slot],
                recv_sem=r_sem.at[slot],
                device_id=target,
                device_id_type=MESH,
            ).start()

    def arrived(slot, sem):
        span = X.at[rows(slot * SLOT, SLOT - 32)]
        pltpu.make_async_copy(span, span, sem.at[slot]).wait()

    def own(slot):
        return [X[pl.ds(slot * SLOT + OWN + t, 8, stride=4), :] for t in range(4)]

    def set_own(slot, value):
        for t in range(4):
            X[pl.ds(slot * SLOT + OWN + t, 8, stride=4), :] = value[t]

    def split_blocks(stage, weights):
        def body(o, _):
            for k in range(4):
                block = stage[o // 2, lax.rem(o, 2), k]
                high = block.astype(bf16)
                weights[o, pl.ds(0, 128), pl.ds(k * 128, 128)] = high
                weights[o, pl.ds(128, 128), pl.ds(k * 128, 128)] = (block - high.astype(f32)).astype(bf16)
            return 0

        lax.fori_loop(0, 8, body, 0)

    upper = lax.broadcasted_iota(jnp.int32, (8, 128), 0) < 4

    def product(slot, weights):
        for pair in range(24):
            x = X[pl.ds(pl.multiple_of(slot * SLOT + pair * 8, 8), 8), :]
            high = x.astype(bf16).astype(f32)
            low = pltpu.roll(x - high, 4, axis=0)
            GB[2 * pair] = jnp.where(upper, high, low)
            GB[2 * pair + 1] = jnp.where(upper, low, high)
        for pair in range(4):
            sums = []
            for o in (2 * pair, 2 * pair + 1):
                lhs = jnp.concatenate(
                    [
                        GB[IDX[o * 4 + k]].astype(bf16)
                        for k in range(4)
                    ],
                    axis=1,
                )
                both = lax.dot_general(
                    lhs, weights[o], (((1,), (1,)), ((), ())), preferred_element_type=f32
                )
                both = both[:, :128] + both[:, 128:]
                sums.append(both + pltpu.roll(both, 4, axis=0))
            PR[pl.ds(pair * 8, 8), :] = jnp.where(upper, sums[0], sums[1])
        return [PR[pl.ds(t, 8, stride=4), :] for t in range(4)]

    def all_sum(step, row):
        RA[step, h_lo] = row

        def send_a(k, _):
            pltpu.make_async_remote_copy(
                src_ref=RA.at[step, h_lo], dst_ref=RA.at[step, h_lo],
                send_sem=rs_sem.at[2 * step], recv_sem=ra_sem.at[step],
                device_id=partner_a(k), device_id_type=MESH,
            ).start()
            return 0

        lax.fori_loop(1, ga, send_a, 0)
        span = RA.at[step, pl.ds(0, ga - 1)]
        pltpu.make_async_copy(span, span, ra_sem.at[step]).wait()
        RB[step, index_b] = jnp.sum(RA[step], axis=0)

        def send_b(k, _):
            pltpu.make_async_remote_copy(
                src_ref=RB.at[step, index_b], dst_ref=RB.at[step, index_b],
                send_sem=rs_sem.at[2 * step + 1], recv_sem=rb_sem.at[step],
                device_id=partner_b(k), device_id_type=MESH,
            ).start()
            return 0

        lax.fori_loop(1, gb, send_b, 0)
        span = RB.at[step, pl.ds(0, gb - 1)]
        pltpu.make_async_copy(span, span, rb_sem.at[step]).wait()
        return jnp.sum(RB[step], axis=0)

    lane = lax.broadcasted_iota(jnp.int32, (1, 128), 1)

    def coefficients(step):
        vectors = [[K[j * 4 + t] for t in range(4)] for j in range(4)]
        pairs = [(i, j) for i in range(4) for j in range(i, 4)]
        row = jnp.zeros((1, 128), f32)
        for number, (i, j) in enumerate(pairs):
            part = sum(vectors[i][t] * vectors[j][t] for t in range(4))
            total = jnp.sum(jnp.sum(part, axis=0, keepdims=True), axis=1, keepdims=True)
            row = jnp.where(lane == number, total, row)
        total = all_sum(step, row)
        gram = {
            pair: jnp.sum(jnp.where(lane == number, total, 0.0), axis=1, keepdims=True)
            for number, pair in enumerate(pairs)
        }
        zero = jnp.zeros((1, 1), f32)
        R = [[zero] * 4 for _ in range(4)]
        for i in range(4):
            pivot = gram[i, i]
            for m in range(i):
                pivot = pivot - R[m][i] * R[m][i]
            pivot = jnp.maximum(pivot, 1e-14 * gram[i, i])
            R[i][i] = jnp.sqrt(pivot)
            inverse = 1.0 / R[i][i]
            for j in range(i + 1, 4):
                value = gram[i, j]
                for m in range(i):
                    value = value - R[m][i] * R[m][j]
                R[i][j] = value * inverse
        hess = [[(SHIFT - 1.0) * R[i][j] + R[i][j + 1] for j in range(3)] for i in range(4)]
        target = [R[0][0], zero, zero, zero]
        for c in range(3):
            top, low = hess[c][c], hess[c + 1][c]
            inverse = 1.0 / jnp.sqrt(top * top + low * low)
            cosine, sine = top * inverse, low * inverse
            for j in range(c, 3):
                top, low = hess[c][j], hess[c + 1][j]
                hess[c][j] = cosine * top + sine * low
                hess[c + 1][j] = cosine * low - sine * top
            top, low = target[c], target[c + 1]
            target[c] = cosine * top + sine * low
            target[c + 1] = cosine * low - sine * top
        answer = [zero] * 3
        for c in (2, 1, 0):
            value = target[c]
            for j in range(c + 1, 3):
                value = value - hess[c][j] * answer[j]
            answer[c] = value / hess[c][c]
        return answer

    def limitation(iron):
        squared = iron * iron
        return squared / (1.0 + squared)

    def slope(iron):
        denominator = 1.0 + iron * iron
        return 2.0 * iron / (denominator * denominator)

    def krylov(first, c, residual):
        forcing, uptake = FU[pl.ds(0, 8), :], FU[pl.ds(8, 8), :]
        flux_one = uptake * limitation(c[3])
        flux_three = uptake * c[1] * slope(c[3])
        for t in range(4):
            K[t] = residual[t]

        def step(j, _):
            v = [K[4 * j + t] for t in range(4)]
            slot = first + 2 * j
            set_own(slot, v)
            exchange(slot)
            change = flux_one * v[1] + flux_three * v[3]
            middle = [
                0.5 * v[0] - 0.5 * forcing * v[0],
                0.5 * v[1] - 0.5 * change,
                0.4 * v[2] + 0.25 * change,
                0.5 * v[3] + 0.5 * forcing * v[0] - 0.025 * change,
            ]
            arrived(slot, r_sem)
            image = product(slot, WA)
            middle = [m + i for m, i in zip(middle, image)]
            set_own(slot + 1, middle)
            exchange(slot + 1)
            arrived(slot + 1, r_sem)
            image = product(slot + 1, WB)
            for t in range(4):
                K[4 * (j + 1) + t] = middle[t] + image[t] - SHIFT * v[t]
            return 0

        lax.fori_loop(0, KRYLOV, step, 0)

    exchange(0)
    exchange(UPTAKE)
    copy_a.wait()
    split_blocks(st_a, WA)
    arrived(0, r_sem)
    image = product(0, WA)
    c = own(0)
    forcing, uptake = FU[pl.ds(0, 8), :], FU[pl.ds(8, 8), :]
    flux = uptake * c[1] * limitation(c[3])
    source = [
        forcing * (1.0 - c[0]),
        -flux,
        0.5 * flux - 0.2 * c[2],
        forcing * c[0] - 0.05 * flux,
    ]
    middle = [0.5 * c[t] + image[t] + 0.5 * source[t] for t in range(4)]
    set_own(1, middle)
    exchange(1)
    copy_b.wait()
    split_blocks(st_b, WB)
    arrived(1, r_sem)
    image = product(1, WB)
    krylov(2, c, [c[t] - middle[t] - image[t] for t in range(4)])
    weights = coefficients(0)

    arrived(UPTAKE, r_sem)

    def wide(slot, t):
        return X[pl.ds(slot * SLOT + t, 48, stride=4), :]

    def wide_sum(first_slot, t):
        return sum(weights[j] * wide(first_slot + 2 * j, t) for j in range(3))

    tracer_old, iron_old = wide(0, 1), wide(0, 3)
    iron_step = wide_sum(2, 3)
    tracer_new, iron_new = tracer_old + wide_sum(2, 1), iron_old + iron_step
    rest = wide(UPTAKE, 0) * (
        tracer_new * (limitation(iron_new) - limitation(iron_old)) - tracer_old * slope(iron_old) * iron_step
    )
    for t in range(4):
        value = wide(1, t) + wide_sum(3, t)
        if t:
            value = value + (0.0, -0.5, 0.25, -0.025)[t] * rest
        X[pl.ds(8 * SLOT + t, 48, stride=4), :] = value
    image = product(8, WB)
    middle = own(8)
    c = [own(0)[t] + sum(weights[j] * K[4 * j + t] for j in range(3)) for t in range(4)]

    krylov(9, c, [c[t] - middle[t] - image[t] for t in range(4)])
    weights = coefficients(1)
    for t in range(4):
        out[pl.ds(t, 8, stride=4), :] = c[t] + sum(weights[j] * K[4 * j + t] for j in range(3))

    for slot in (0, 1, 2, 3, 4, 5, 6, 7, 9, 10, 11, 12, 13, 14, UPTAKE):
        arrived(slot, s_sem)
    for step in range(NEWTON):
        span = RA.at[step, pl.ds(0, ga - 1)]
        pltpu.make_async_copy(span, span, rs_sem.at[2 * step]).wait()
        span = RB.at[step, pl.ds(0, gb - 1)]
        pltpu.make_async_copy(span, span, rs_sem.at[2 * step + 1]).wait()


def per_device(nh, nd, state, explicit_blocks, implicit_blocks, pattern, cavity_mask, melt_rate, uptake_rate):
    ga = 16 if nh % 16 == 0 else 2
    gb = (nh // ga) * nd
    vmem = pl.BlockSpec(memory_space=pltpu.VMEM)
    result = pl.pallas_call(
        functools.partial(kernel, nh, nd, ga),
        out_shape=jax.ShapeDtypeStruct((32, 128), f32),
        in_specs=[pl.BlockSpec(memory_space=pltpu.HBM)] * 7,
        out_specs=vmem,
        scratch_shapes=[
            pltpu.VMEM((4, 4, 2, 128), f32),
            pltpu.SMEM((4, 2, 4), jnp.int32),
            pltpu.VMEM((4, 2, 128), jnp.int32),
            pltpu.VMEM((4, 2, 128), f32),
            pltpu.VMEM((4, 2, 128), f32),
            pltpu.VMEM((SLOTS * SLOT + 32, 128), f32),
            pltpu.VMEM((48, 8, 128), f32),
            pltpu.SMEM((32,), jnp.int32),
            pltpu.VMEM((4, 2, 4, 128, 128), f32),
            pltpu.VMEM((4, 2, 4, 128, 128), f32),
            pltpu.VMEM((8, 256, 512), bf16),
            pltpu.VMEM((8, 256, 512), bf16),
            pltpu.VMEM((32, 128), f32),
            pltpu.VMEM((16, 128), f32),
            pltpu.VMEM((16, 8, 128), f32),
            pltpu.VMEM((NEWTON, ga, 1, 128), f32),
            pltpu.VMEM((NEWTON, gb, 1, 128), f32),
            pltpu.SemaphoreType.DMA((7,)),
            pltpu.SemaphoreType.DMA((SLOTS,)),
            pltpu.SemaphoreType.DMA((SLOTS,)),
            pltpu.SemaphoreType.DMA((NEWTON,)),
            pltpu.SemaphoreType.DMA((NEWTON,)),
            pltpu.SemaphoreType.DMA((2 * NEWTON,)),
        ],
        compiler_params=pltpu.CompilerParams(
            collective_id=0, has_side_effects=True, vmem_limit_bytes=24 * 1024 * 1024
        ),
    )(state, explicit_blocks, implicit_blocks, pattern, cavity_mask, melt_rate, uptake_rate)
    return result.reshape(4, 2, 4, 128).transpose(2, 0, 1, 3)


def solution(mesh):
    nh, nd = mesh.shape["horiz"], mesh.shape["depth"]
    return jax.shard_map(
        functools.partial(per_device, nh, nd),
        mesh=mesh,
        in_specs=(
            P(None, "horiz", "depth", None),
            P("horiz", "depth", None, None, None),
            P("horiz", "depth", None, None, None),
            P("horiz", "depth", None),
            P("horiz", "depth", None),
            P("horiz", "depth", None),
            P("horiz", "depth", None),
        ),
        out_specs=P(None, "horiz", "depth", None),
        check_vma=False,
    )
```

```python
import functools
import jax
import jax.numpy as jnp
from jax import lax
from jax.experimental import pallas as pl
from jax.experimental.pallas import tpu as pltpu
from jax.sharding import PartitionSpec as P

NEWTON = 2
KRYLOV = 3
SHIFT = 0.3

f32 = jnp.float32
bf16 = jnp.bfloat16
MESH = pl.DeviceIdType.MESH

SLOT = 192
OWN = 80
UPTAKE = 15
SLOTS = 16
ZERO = SLOTS * SLOT

DIRECTIONS = [(1, 1), (-1, 1), (1, -1), (-1, -1), (0, 1), (0, -1), (1, 0), (-1, 0)]


def rows(start, size):
    return pl.ds(pl.multiple_of(start, 16) if not isinstance(start, int) else start, size)


def kernel(
    nh, nd, ga, c_hbm, a_hbm, b_hbm, pat_hbm, mask_hbm, melt_hbm, upt_hbm, out,
    c_in, pat, mask, melt, upt, X, GB, IDX, st_a, st_b, WA, WB, PR, FU, K, RA, RB,
    w_sem, r_sem, s_sem, ra_sem, rb_sem, rs_sem,
):
    gb = (nh // ga) * nd
    h = lax.axis_index("horiz")
    d = lax.axis_index("depth")

    h_hi = h // ga
    h_lo = lax.rem(h, ga)
    index_b = h_hi * nd + d

    sends = []
    for sh, sd in DIRECTIONS:
        n_rows = 16 if sh else 32
        src_h = {1: 4, -1: 2, 0: 2}[sh]
        dst_h = {1: 0, -1: 6, 0: 2}[sh]
        in_h = jnp.logical_and(h + sh >= 0, h + sh < nh)
        in_d = jnp.logical_and(d + sd >= 0, d + sd < nd)
        other_d = d + 1 - 2 * lax.rem(d, 2)
        other_h = h + 1 - 2 * lax.rem(h, 2)
        near_h = h + sh if sh else other_h
        target = (
            jnp.where(in_h, jnp.where(in_d, h + sh, near_h), h),
            jnp.where(in_h, jnp.where(in_d, d + sd, d), other_d),
        )
        far_h = {1: 6, -1: 0, 0: 2}[sh]
        position = jnp.where(
            in_h,
            jnp.where(in_d, (1 - sd) * 16 + dst_h * 2, (1 + sd) * 16 + dst_h * 2),
            (1 - sd) * 16 + far_h * 2,
        )
        sends.append((jnp.logical_and(in_h, in_d), (16 + src_h * 2) * 4, position * 4, n_rows, target))

    nx = nh // ga
    far = lambda k, n: min(k, n - k)
    partners_a = [
        (h_hi * ga + lax.rem(h_lo + k, ga), d)
        for k in sorted(range(1, ga), key=lambda k: -far(k, ga))
    ]
    partners_b = [
        (lax.rem(h_hi + i, nx) * ga + h_lo, lax.rem(d + j, nd))
        for i, j in sorted(
            [(i, j) for i in range(nx) for j in range(nd) if i + j],
            key=lambda ij: -(far(ij[0], nx) + far(ij[1], nd)),
        )
    ]

    barrier = pltpu.get_barrier_semaphore()
    for target in partners_a + partners_b + [target for *_, target in sends]:
        pl.semaphore_signal(barrier, inc=1, device_id=target, device_id_type=MESH)

    small = [
        pltpu.make_async_copy(source, target, w_sem.at[2 + number])
        for number, (source, target) in enumerate(
            [(c_hbm, c_in), (upt_hbm, upt), (pat_hbm, pat), (mask_hbm, mask), (melt_hbm, melt)]
        )
    ]
    for copy in small:
        copy.start()
    copy_a = pltpu.make_async_copy(a_hbm, st_a, w_sem.at[0])
    copy_b = pltpu.make_async_copy(b_hbm, st_b, w_sem.at[1])
    copy_a.start()
    copy_b.start()

    for copy in small:
        copy.wait()
    for hh in range(4):
        for dd in range(2):
            o = hh * 2 + dd
            for t in range(4):
                X[pl.ds(OWN + o * 4 + t, 1), :] = c_in[t, hh, pl.ds(dd, 1), :]
            u_row = upt[hh, pl.ds(dd, 1), :]
            X[pl.ds(UPTAKE * SLOT + OWN + o * 4, 4), :] = jnp.broadcast_to(u_row, (4, 128))
            FU[pl.ds(o, 1), :] = mask[hh, pl.ds(dd, 1), :].astype(f32) * melt[hh, pl.ds(dd, 1), :]
            FU[pl.ds(8 + o, 1), :] = u_row
    X[pl.ds(ZERO, 32), :] = jnp.zeros((32, 128), f32)

    for o in range(8):
        for k in range(4):
            code = pat[o // 2, o % 2, k]
            five = lax.div(code, 5)
            row = (o // 2) + five
            dep = (o % 2) + code - 5 * five
            band = lax.div(dep, 2)
            IDX[o * 4 + k] = band * 16 + row * 2 + dep - 2 * band

    pl.semaphore_wait(barrier, 8 + (ga - 1) + (gb - 1))

    def exchange(slot):
        base = slot * SLOT
        for inside, src, dst, n_rows, target in sends:
            pltpu.make_async_remote_copy(
                src_ref=X.at[rows(jnp.where(inside, base + src, ZERO), n_rows)],
                dst_ref=X.at[rows(base + dst, n_rows)],
                send_sem=s_sem.at[slot],
                recv_sem=r_sem.at[slot],
                device_id=target,
                device_id_type=MESH,
            ).start()

    def arrived(slot, sem):
        span = X.at[rows(slot * SLOT, SLOT - 32)]
        pltpu.make_async_copy(span, span, sem.at[slot]).wait()

    def own(slot):
        return [X[pl.ds(slot * SLOT + OWN + t, 8, stride=4), :] for t in range(4)]

    def set_own(slot, value):
        for t in range(4):
            X[pl.ds(slot * SLOT + OWN + t, 8, stride=4), :] = value[t]

    def split_blocks(stage, weights):
        def body(o, _):
            for k in range(4):
                block = stage[o // 2, lax.rem(o, 2), k].T
                high = block.astype(bf16)
                weights[o, pl.ds(k * 128, 128), pl.ds(0, 128)] = high
                weights[o, pl.ds(k * 128, 128), pl.ds(128, 128)] = (block - high.astype(f32)).astype(bf16)
            return 0

        lax.fori_loop(0, 8, body, 0)

    upper = lax.broadcasted_iota(jnp.int32, (8, 128), 0) < 4

    def product(slot, weights):
        for pair in range(24):
            x = X[pl.ds(pl.multiple_of(slot * SLOT + pair * 8, 8), 8), :]
            high = x.astype(bf16).astype(f32)
            low = pltpu.roll(x - high, 4, axis=0)
            GB[2 * pair] = jnp.where(upper, high, low)
            GB[2 * pair + 1] = jnp.where(upper, low, high)
        for pair in range(4):
            sums = []
            for o in (2 * pair, 2 * pair + 1):
                lhs = jnp.concatenate(
                    [
                        GB[IDX[o * 4 + k]].astype(bf16)
                        for k in range(4)
                    ],
                    axis=1,
                )
                both = lax.dot_general(
                    lhs, weights[o], (((1,), (0,)), ((), ())), preferred_element_type=f32
                )
                both = both[:, :128] + both[:, 128:]
                sums.append(both + pltpu.roll(both, 4, axis=0))
            PR[pl.ds(pair * 8, 8), :] = jnp.where(upper, sums[0], sums[1])
        return [PR[pl.ds(t, 8, stride=4), :] for t in range(4)]

    def all_sum(step, row):
        RA[step, h_lo] = row

        for target in partners_a:
            pltpu.make_async_remote_copy(
                src_ref=RA.at[step, h_lo], dst_ref=RA.at[step, h_lo],
                send_sem=rs_sem.at[2 * step], recv_sem=ra_sem.at[step],
                device_id=target, device_id_type=MESH,
            ).start()
        span = RA.at[step, pl.ds(0, ga - 1)]
        pltpu.make_async_copy(span, span, ra_sem.at[step]).wait()
        RB[step, index_b] = jnp.sum(RA[step], axis=0)

        for target in partners_b:
            pltpu.make_async_remote_copy(
                src_ref=RB.at[step, index_b], dst_ref=RB.at[step, index_b],
                send_sem=rs_sem.at[2 * step + 1], recv_sem=rb_sem.at[step],
                device_id=target, device_id_type=MESH,
            ).start()
        span = RB.at[step, pl.ds(0, gb - 1)]
        pltpu.make_async_copy(span, span, rb_sem.at[step]).wait()
        return jnp.sum(RB[step], axis=0)

    lane = lax.broadcasted_iota(jnp.int32, (1, 128), 1)

    def coefficients(step):
        vectors = [[K[j * 4 + t] for t in range(4)] for j in range(4)]
        pairs = [(i, j) for i in range(4) for j in range(i, 4)]
        row = jnp.zeros((1, 128), f32)
        for number, (i, j) in enumerate(pairs):
            part = sum(vectors[i][t] * vectors[j][t] for t in range(4))
            total = jnp.sum(jnp.sum(part, axis=0, keepdims=True), axis=1, keepdims=True)
            row = jnp.where(lane == number, total, row)
        total = all_sum(step, row)
        gram = {
            pair: jnp.sum(jnp.where(lane == number, total, 0.0), axis=1, keepdims=True)
            for number, pair in enumerate(pairs)
        }
        zero = jnp.zeros((1, 1), f32)
        R = [[zero] * 4 for _ in range(4)]
        for i in range(4):
            pivot = gram[i, i]
            for m in range(i):
                pivot = pivot - R[m][i] * R[m][i]
            pivot = jnp.maximum(pivot, 1e-14 * gram[i, i])
            R[i][i] = jnp.sqrt(pivot)
            inverse = 1.0 / R[i][i]
            for j in range(i + 1, 4):
                value = gram[i, j]
                for m in range(i):
                    value = value - R[m][i] * R[m][j]
                R[i][j] = value * inverse
        hess = [[(SHIFT - 1.0) * R[i][j] + R[i][j + 1] for j in range(3)] for i in range(4)]
        target = [R[0][0], zero, zero, zero]
        for c in range(3):
            top, low = hess[c][c], hess[c + 1][c]
            inverse = 1.0 / jnp.sqrt(top * top + low * low)
            cosine, sine = top * inverse, low * inverse
            for j in range(c, 3):
                top, low = hess[c][j], hess[c + 1][j]
                hess[c][j] = cosine * top + sine * low
                hess[c + 1][j] = cosine * low - sine * top
            top, low = target[c], target[c + 1]
            target[c] = cosine * top + sine * low
            target[c + 1] = cosine * low - sine * top
        answer = [zero] * 3
        for c in (2, 1, 0):
            value = target[c]
            for j in range(c + 1, 3):
                value = value - hess[c][j] * answer[j]
            answer[c] = value / hess[c][c]
        return answer

    def limitation(iron):
        squared = iron * iron
        return squared / (1.0 + squared)

    def slope(iron):
        denominator = 1.0 + iron * iron
        return 2.0 * iron / (denominator * denominator)

    def krylov(first, c, residual):
        forcing, uptake = FU[pl.ds(0, 8), :], FU[pl.ds(8, 8), :]
        flux_one = uptake * limitation(c[3])
        flux_three = uptake * c[1] * slope(c[3])
        for t in range(4):
            K[t] = residual[t]

        def step(j, _):
            v = [K[4 * j + t] for t in range(4)]
            slot = first + 2 * j
            set_own(slot, v)
            exchange(slot)
            change = flux_one * v[1] + flux_three * v[3]
            middle = [
                0.5 * v[0] - 0.5 * forcing * v[0],
                0.5 * v[1] - 0.5 * change,
                0.4 * v[2] + 0.25 * change,
                0.5 * v[3] + 0.5 * forcing * v[0] - 0.025 * change,
            ]
            arrived(slot, r_sem)
            image = product(slot, WA)
            middle = [m + i for m, i in zip(middle, image)]
            set_own(slot + 1, middle)
            exchange(slot + 1)
            arrived(slot + 1, r_sem)
            image = product(slot + 1, WB)
            for t in range(4):
                K[4 * (j + 1) + t] = middle[t] + image[t] - SHIFT * v[t]
            return 0

        lax.fori_loop(0, KRYLOV, step, 0)

    exchange(0)
    exchange(UPTAKE)
    copy_a.wait()
    split_blocks(st_a, WA)
    arrived(0, r_sem)
    image = product(0, WA)
    c = own(0)
    forcing, uptake = FU[pl.ds(0, 8), :], FU[pl.ds(8, 8), :]
    flux = uptake * c[1] * limitation(c[3])
    source = [
        forcing * (1.0 - c[0]),
        -flux,
        0.5 * flux - 0.2 * c[2],
        forcing * c[0] - 0.05 * flux,
    ]
    middle = [0.5 * c[t] + image[t] + 0.5 * source[t] for t in range(4)]
    set_own(1, middle)
    exchange(1)
    copy_b.wait()
    split_blocks(st_b, WB)
    arrived(1, r_sem)
    image = product(1, WB)
    krylov(2, c, [c[t] - middle[t] - image[t] for t in range(4)])
    weights = coefficients(0)

    arrived(UPTAKE, r_sem)

    def wide(slot, t):
        return X[pl.ds(slot * SLOT + t, 48, stride=4), :]

    def wide_sum(first_slot, t):
        return sum(weights[j] * wide(first_slot + 2 * j, t) for j in range(3))

    tracer_old, iron_old = wide(0, 1), wide(0, 3)
    iron_step = wide_sum(2, 3)
    tracer_new, iron_new = tracer_old + wide_sum(2, 1), iron_old + iron_step
    rest = wide(UPTAKE, 0) * (
        tracer_new * (limitation(iron_new) - limitation(iron_old)) - tracer_old * slope(iron_old) * iron_step
    )
    for t in range(4):
        value = wide(1, t) + wide_sum(3, t)
        if t:
            value = value + (0.0, -0.5, 0.25, -0.025)[t] * rest
        X[pl.ds(8 * SLOT + t, 48, stride=4), :] = value
    image = product(8, WB)
    middle = own(8)
    c = [own(0)[t] + sum(weights[j] * K[4 * j + t] for j in range(3)) for t in range(4)]

    krylov(9, c, [c[t] - middle[t] - image[t] for t in range(4)])
    weights = coefficients(1)
    for t in range(4):
        out[pl.ds(t, 8, stride=4), :] = c[t] + sum(weights[j] * K[4 * j + t] for j in range(3))

    for slot in (0, 1, 2, 3, 4, 5, 6, 7, 9, 10, 11, 12, 13, 14, UPTAKE):
        arrived(slot, s_sem)
    for step in range(NEWTON):
        span = RA.at[step, pl.ds(0, ga - 1)]
        pltpu.make_async_copy(span, span, rs_sem.at[2 * step]).wait()
        span = RB.at[step, pl.ds(0, gb - 1)]
        pltpu.make_async_copy(span, span, rs_sem.at[2 * step + 1]).wait()


def per_device(nh, nd, state, explicit_blocks, implicit_blocks, pattern, cavity_mask, melt_rate, uptake_rate):
    ga = 16 if nh % 16 == 0 else 2
    gb = (nh // ga) * nd
    vmem = pl.BlockSpec(memory_space=pltpu.VMEM)
    result = pl.pallas_call(
        functools.partial(kernel, nh, nd, ga),
        out_shape=jax.ShapeDtypeStruct((32, 128), f32),
        in_specs=[pl.BlockSpec(memory_space=pltpu.HBM)] * 7,
        out_specs=vmem,
        scratch_shapes=[
            pltpu.VMEM((4, 4, 2, 128), f32),
            pltpu.SMEM((4, 2, 4), jnp.int32),
            pltpu.VMEM((4, 2, 128), jnp.int32),
            pltpu.VMEM((4, 2, 128), f32),
            pltpu.VMEM((4, 2, 128), f32),
            pltpu.VMEM((SLOTS * SLOT + 32, 128), f32),
            pltpu.VMEM((48, 8, 128), f32),
            pltpu.SMEM((32,), jnp.int32),
            pltpu.VMEM((4, 2, 4, 128, 128), f32),
            pltpu.VMEM((4, 2, 4, 128, 128), f32),
            pltpu.VMEM((8, 512, 256), bf16),
            pltpu.VMEM((8, 512, 256), bf16),
            pltpu.VMEM((32, 128), f32),
            pltpu.VMEM((16, 128), f32),
            pltpu.VMEM((16, 8, 128), f32),
            pltpu.VMEM((NEWTON, ga, 1, 128), f32),
            pltpu.VMEM((NEWTON, gb, 1, 128), f32),
            pltpu.SemaphoreType.DMA((7,)),
            pltpu.SemaphoreType.DMA((SLOTS,)),
            pltpu.SemaphoreType.DMA((SLOTS,)),
            pltpu.SemaphoreType.DMA((NEWTON,)),
            pltpu.SemaphoreType.DMA((NEWTON,)),
            pltpu.SemaphoreType.DMA((2 * NEWTON,)),
        ],
        compiler_params=pltpu.CompilerParams(
            collective_id=0, has_side_effects=True, vmem_limit_bytes=63 * 1024 * 1024
        ),
    )(state, explicit_blocks, implicit_blocks, pattern, cavity_mask, melt_rate, uptake_rate)
    return result.reshape(4, 2, 4, 128).transpose(2, 0, 1, 3)


def solution(mesh):
    nh, nd = mesh.shape["horiz"], mesh.shape["depth"]
    return jax.shard_map(
        functools.partial(per_device, nh, nd),
        mesh=mesh,
        in_specs=(
            P(None, "horiz", "depth", None),
            P("horiz", "depth", None, None, None),
            P("horiz", "depth", None, None, None),
            P("horiz", "depth", None),
            P("horiz", "depth", None),
            P("horiz", "depth", None),
            P("horiz", "depth", None),
        ),
        out_specs=P(None, "horiz", "depth", None),
        check_vma=False,
    )
```

```python
import functools
import jax
import jax.numpy as jnp
from jax import lax
from jax.experimental import pallas as pl
from jax.experimental.pallas import tpu as pltpu
from jax.sharding import PartitionSpec as P

NEWTON = 2
KRYLOV = 3
SHIFT = 0.3

f32 = jnp.float32
bf16 = jnp.bfloat16
MESH = pl.DeviceIdType.MESH

SLOT = 192
OWN = 80
UPTAKE = 15
SLOTS = 16
ZERO = SLOTS * SLOT

DIRECTIONS = [(1, 1), (1, -1), (1, 0), (0, 1), (0, -1), (-1, 1), (-1, -1), (-1, 0)]


def rows(start, size):
    return pl.ds(pl.multiple_of(start, 16) if not isinstance(start, int) else start, size)


def kernel(
    nh, nd, ga, c_hbm, a_hbm, b_hbm, pat_hbm, mask_hbm, melt_hbm, upt_hbm, out,
    c_in, pat, mask, melt, upt, X, GB, IDX, st_a, st_b, WA, WB, PR, FU, K, RA, RB,
    w_sem, r_sem, o_sem, s_sem, ra_sem, rb_sem, rs_sem,
):
    gb = (nh // ga) * nd
    h = lax.axis_index("horiz")
    d = lax.axis_index("depth")

    h_hi = h // ga
    h_lo = lax.rem(h, ga)
    index_b = h_hi * nd + d

    sends = []
    outward = 2 * lax.rem(h, 2) - 1
    for side, sd in DIRECTIONS:
        n_rows = 16 if side else 32
        sh = side * outward
        src_h = 3 + sh if side else 2
        dst_h = 3 - 3 * sh if side else 2
        in_h = jnp.logical_and(h + sh >= 0, h + sh < nh)
        in_d = jnp.logical_and(d + sd >= 0, d + sd < nd)
        other_d = d + 1 - 2 * lax.rem(d, 2)
        other_h = h + 1 - 2 * lax.rem(h, 2)
        near_h = h + sh if side else other_h
        target = (
            jnp.where(in_h, jnp.where(in_d, h + sh, near_h), h),
            jnp.where(in_h, jnp.where(in_d, d + sd, d), other_d),
        )
        far_h = 3 + 3 * sh if side else 2
        position = jnp.where(
            in_h,
            jnp.where(in_d, (1 - sd) * 16 + dst_h * 2, (1 + sd) * 16 + dst_h * 2),
            (1 - sd) * 16 + far_h * 2,
        )
        sends.append((jnp.logical_and(in_h, in_d), (16 + src_h * 2) * 4, position * 4, n_rows, target, side == 1))

    nx = nh // ga
    far = lambda k, n: min(k, n - k)
    other_lo = h_lo + 1 - 2 * lax.rem(h_lo, 2)
    partners_a = [
        (h_hi * ga + lax.rem(h_lo + k, ga), d)
        for k in sorted(range(1, ga), key=lambda k: -far(k, ga))
    ]
    partners_b = [
        (lax.rem(h_hi + i, nx) * ga + other_lo, lax.rem(d + j, nd))
        for i, j in sorted(
            [(i, j) for i in range(nx) for j in range(nd) if i + j],
            key=lambda ij: -(far(ij[0], nx) + far(ij[1], nd)),
        )
    ]

    barrier = pltpu.get_barrier_semaphore()
    halo = [target for *_, target, _ in sends]
    for target in partners_a[:3] + halo[:3] + partners_b[:5] + partners_a[3:7] + halo[3:] + partners_b[5:] + partners_a[7:]:
        pl.semaphore_signal(barrier, inc=1, device_id=target, device_id_type=MESH)

    small = [
        pltpu.make_async_copy(source, target, w_sem.at[2 + number])
        for number, (source, target) in enumerate(
            [(c_hbm, c_in), (upt_hbm, upt), (pat_hbm, pat), (mask_hbm, mask), (melt_hbm, melt)]
        )
    ]
    for copy in small:
        copy.start()
    copy_a = pltpu.make_async_copy(a_hbm, st_a, w_sem.at[0])
    copy_b = pltpu.make_async_copy(b_hbm, st_b, w_sem.at[1])
    copy_a.start()
    copy_b.start()

    for copy in small:
        copy.wait()
    for hh in range(4):
        for dd in range(2):
            o = hh * 2 + dd
            for t in range(4):
                X[pl.ds(OWN + o * 4 + t, 1), :] = c_in[t, hh, pl.ds(dd, 1), :]
            u_row = upt[hh, pl.ds(dd, 1), :]
            X[pl.ds(UPTAKE * SLOT + OWN + o * 4, 4), :] = jnp.broadcast_to(u_row, (4, 128))
            FU[pl.ds(o, 1), :] = mask[hh, pl.ds(dd, 1), :].astype(f32) * melt[hh, pl.ds(dd, 1), :]
            FU[pl.ds(8 + o, 1), :] = u_row
    X[pl.ds(ZERO, 32), :] = jnp.zeros((32, 128), f32)

    for o in range(8):
        for k in range(4):
            code = pat[o // 2, o % 2, k]
            five = lax.div(code, 5)
            row = (o // 2) + five
            dep = (o % 2) + code - 5 * five
            band = lax.div(dep, 2)
            IDX[o * 4 + k] = band * 16 + row * 2 + dep - 2 * band

    pl.semaphore_wait(barrier, 8 + (ga - 1) + (gb - 1))

    def exchange(slot):
        base = slot * SLOT
        for inside, src, dst, n_rows, target, outer in sends:
            pltpu.make_async_remote_copy(
                src_ref=X.at[rows(jnp.where(inside, base + src, ZERO), n_rows)],
                dst_ref=X.at[rows(base + dst, n_rows)],
                send_sem=s_sem.at[slot],
                recv_sem=(o_sem if outer else r_sem).at[slot],
                device_id=target,
                device_id_type=MESH,
            ).start()

    def finished(slot, sem, size):
        span = X.at[rows(slot * SLOT, size)]
        pltpu.make_async_copy(span, span, sem.at[slot]).wait()

    def own(slot):
        return [X[pl.ds(slot * SLOT + OWN + t, 8, stride=4), :] for t in range(4)]

    def set_own(slot, value):
        for t in range(4):
            X[pl.ds(slot * SLOT + OWN + t, 8, stride=4), :] = value[t]

    def split_blocks(stage, weights):
        def body(o, _):
            for k in range(4):
                block = stage[o // 2, lax.rem(o, 2), k].T
                high = block.astype(bf16)
                weights[o, pl.ds(k * 128, 128), pl.ds(0, 128)] = high
                weights[o, pl.ds(k * 128, 128), pl.ds(128, 128)] = (block - high.astype(f32)).astype(bf16)
            return 0

        lax.fori_loop(0, 8, body, 0)

    upper = lax.broadcasted_iota(jnp.int32, (8, 128), 0) < 4

    core = lax.rem(h, 2)
    inner_rows = (1 - core) * 16
    outer_rows = core * 48

    def spread(slot, first, tiles):
        for band in range(3):
            for i in range(tiles):
                row = band * 64 + first + i * 8
                x = X[pl.ds(pl.multiple_of(slot * SLOT + row, 8), 8), :]
                high = x.astype(bf16).astype(f32)
                low = pltpu.roll(x - high, 4, axis=0)
                place = lax.div(row, 4)
                GB[place] = jnp.where(upper, high, low)
                GB[place + 1] = jnp.where(upper, low, high)

    def half_product(weights, first):
        for pair in range(2):
            sums = []
            for o in (first + 2 * pair, first + 2 * pair + 1):
                lhs = jnp.concatenate([GB[IDX[o * 4 + k]].astype(bf16) for k in range(4)], axis=1)
                both = lax.dot_general(
                    lhs, weights[o], (((1,), (0,)), ((), ())), preferred_element_type=f32
                )
                both = both[:, :128] + both[:, 128:]
                sums.append(both + pltpu.roll(both, 4, axis=0))
            PR[pl.ds(pl.multiple_of(first * 4 + pair * 8, 8), 8), :] = jnp.where(upper, sums[0], sums[1])

    def product(slot, weights, remote=True):
        if remote:
            finished(slot, r_sem, 112)
        spread(slot, inner_rows, 6)
        half_product(weights, 4 * (1 - core))
        if remote:
            finished(slot, o_sem, 48)
        spread(slot, outer_rows, 2)
        half_product(weights, 4 * core)
        return [PR[pl.ds(t, 8, stride=4), :] for t in range(4)]

    def all_sum(step, row):
        RA[step, h_lo] = row

        for target in partners_a:
            pltpu.make_async_remote_copy(
                src_ref=RA.at[step, h_lo], dst_ref=RA.at[step, h_lo],
                send_sem=rs_sem.at[2 * step], recv_sem=ra_sem.at[step],
                device_id=target, device_id_type=MESH,
            ).start()
        span = RA.at[step, pl.ds(0, ga - 1)]
        pltpu.make_async_copy(span, span, ra_sem.at[step]).wait()
        RB[step, index_b] = jnp.sum(RA[step], axis=0)

        for target in partners_b:
            pltpu.make_async_remote_copy(
                src_ref=RB.at[step, index_b], dst_ref=RB.at[step, index_b],
                send_sem=rs_sem.at[2 * step + 1], recv_sem=rb_sem.at[step],
                device_id=target, device_id_type=MESH,
            ).start()
        span = RB.at[step, pl.ds(0, gb - 1)]
        pltpu.make_async_copy(span, span, rb_sem.at[step]).wait()
        return jnp.sum(RB[step], axis=0)

    lane = lax.broadcasted_iota(jnp.int32, (1, 128), 1)

    def coefficients(step):
        vectors = [[K[j * 4 + t] for t in range(4)] for j in range(4)]
        pairs = [(i, j) for i in range(4) for j in range(i, 4)]
        row = jnp.zeros((1, 128), f32)
        for number, (i, j) in enumerate(pairs):
            part = sum(vectors[i][t] * vectors[j][t] for t in range(4))
            total = jnp.sum(jnp.sum(part, axis=0, keepdims=True), axis=1, keepdims=True)
            row = jnp.where(lane == number, total, row)
        total = all_sum(step, row)
        gram = {
            pair: jnp.sum(jnp.where(lane == number, total, 0.0), axis=1, keepdims=True)
            for number, pair in enumerate(pairs)
        }
        zero = jnp.zeros((1, 1), f32)
        R = [[zero] * 4 for _ in range(4)]
        for i in range(4):
            pivot = gram[i, i]
            for m in range(i):
                pivot = pivot - R[m][i] * R[m][i]
            pivot = jnp.maximum(pivot, 1e-14 * gram[i, i])
            R[i][i] = jnp.sqrt(pivot)
            inverse = 1.0 / R[i][i]
            for j in range(i + 1, 4):
                value = gram[i, j]
                for m in range(i):
                    value = value - R[m][i] * R[m][j]
                R[i][j] = value * inverse
        hess = [[(SHIFT - 1.0) * R[i][j] + R[i][j + 1] for j in range(3)] for i in range(4)]
        target = [R[0][0], zero, zero, zero]
        for c in range(3):
            top, low = hess[c][c], hess[c + 1][c]
            inverse = 1.0 / jnp.sqrt(top * top + low * low)
            cosine, sine = top * inverse, low * inverse
            for j in range(c, 3):
                top, low = hess[c][j], hess[c + 1][j]
                hess[c][j] = cosine * top + sine * low
                hess[c + 1][j] = cosine * low - sine * top
            top, low = target[c], target[c + 1]
            target[c] = cosine * top + sine * low
            target[c + 1] = cosine * low - sine * top
        answer = [zero] * 3
        for c in (2, 1, 0):
            value = target[c]
            for j in range(c + 1, 3):
                value = value - hess[c][j] * answer[j]
            answer[c] = value / hess[c][c]
        return answer

    def limitation(iron):
        squared = iron * iron
        return squared / (1.0 + squared)

    def slope(iron):
        denominator = 1.0 + iron * iron
        return 2.0 * iron / (denominator * denominator)

    def krylov(first, c, residual):
        forcing, uptake = FU[pl.ds(0, 8), :], FU[pl.ds(8, 8), :]
        flux_one = uptake * limitation(c[3])
        flux_three = uptake * c[1] * slope(c[3])
        for t in range(4):
            K[t] = residual[t]

        def step(j, _):
            v = [K[4 * j + t] for t in range(4)]
            slot = first + 2 * j
            set_own(slot, v)
            exchange(slot)
            change = flux_one * v[1] + flux_three * v[3]
            middle = [
                0.5 * v[0] - 0.5 * forcing * v[0],
                0.5 * v[1] - 0.5 * change,
                0.4 * v[2] + 0.25 * change,
                0.5 * v[3] + 0.5 * forcing * v[0] - 0.025 * change,
            ]
            image = product(slot, WA)
            middle = [m + i for m, i in zip(middle, image)]
            set_own(slot + 1, middle)
            exchange(slot + 1)
            image = product(slot + 1, WB)
            for t in range(4):
                K[4 * (j + 1) + t] = middle[t] + image[t] - SHIFT * v[t]
            return 0

        lax.fori_loop(0, KRYLOV, step, 0)

    exchange(0)
    exchange(UPTAKE)
    copy_a.wait()
    split_blocks(st_a, WA)
    image = product(0, WA)
    c = own(0)
    forcing, uptake = FU[pl.ds(0, 8), :], FU[pl.ds(8, 8), :]
    flux = uptake * c[1] * limitation(c[3])
    source = [
        forcing * (1.0 - c[0]),
        -flux,
        0.5 * flux - 0.2 * c[2],
        forcing * c[0] - 0.05 * flux,
    ]
    middle = [0.5 * c[t] + image[t] + 0.5 * source[t] for t in range(4)]
    set_own(1, middle)
    exchange(1)
    copy_b.wait()
    split_blocks(st_b, WB)
    image = product(1, WB)
    krylov(2, c, [c[t] - middle[t] - image[t] for t in range(4)])
    weights = coefficients(0)

    finished(UPTAKE, r_sem, 112)
    finished(UPTAKE, o_sem, 48)

    def wide(slot, t):
        return X[pl.ds(slot * SLOT + t, 48, stride=4), :]

    def wide_sum(first_slot, t):
        return sum(weights[j] * wide(first_slot + 2 * j, t) for j in range(3))

    tracer_old, iron_old = wide(0, 1), wide(0, 3)
    iron_step = wide_sum(2, 3)
    tracer_new, iron_new = tracer_old + wide_sum(2, 1), iron_old + iron_step
    rest = wide(UPTAKE, 0) * (
        tracer_new * (limitation(iron_new) - limitation(iron_old)) - tracer_old * slope(iron_old) * iron_step
    )
    for t in range(4):
        value = wide(1, t) + wide_sum(3, t)
        if t:
            value = value + (0.0, -0.5, 0.25, -0.025)[t] * rest
        X[pl.ds(8 * SLOT + t, 48, stride=4), :] = value
    image = product(8, WB, remote=False)
    middle = own(8)
    c = [own(0)[t] + sum(weights[j] * K[4 * j + t] for j in range(3)) for t in range(4)]

    krylov(9, c, [c[t] - middle[t] - image[t] for t in range(4)])
    weights = coefficients(1)
    for t in range(4):
        out[pl.ds(t, 8, stride=4), :] = c[t] + sum(weights[j] * K[4 * j + t] for j in range(3))

    for slot in (0, 1, 2, 3, 4, 5, 6, 7, 9, 10, 11, 12, 13, 14, UPTAKE):
        finished(slot, s_sem, 160)
    for step in range(NEWTON):
        span = RA.at[step, pl.ds(0, ga - 1)]
        pltpu.make_async_copy(span, span, rs_sem.at[2 * step]).wait()
        span = RB.at[step, pl.ds(0, gb - 1)]
        pltpu.make_async_copy(span, span, rs_sem.at[2 * step + 1]).wait()


def per_device(nh, nd, state, explicit_blocks, implicit_blocks, pattern, cavity_mask, melt_rate, uptake_rate):
    ga = 16 if nh % 16 == 0 else 2
    gb = (nh // ga) * nd
    vmem = pl.BlockSpec(memory_space=pltpu.VMEM)
    result = pl.pallas_call(
        functools.partial(kernel, nh, nd, ga),
        out_shape=jax.ShapeDtypeStruct((32, 128), f32),
        in_specs=[pl.BlockSpec(memory_space=pltpu.HBM)] * 7,
        out_specs=vmem,
        scratch_shapes=[
            pltpu.VMEM((4, 4, 2, 128), f32),
            pltpu.SMEM((4, 2, 4), jnp.int32),
            pltpu.VMEM((4, 2, 128), jnp.int32),
            pltpu.VMEM((4, 2, 128), f32),
            pltpu.VMEM((4, 2, 128), f32),
            pltpu.VMEM((SLOTS * SLOT + 32, 128), f32),
            pltpu.VMEM((48, 8, 128), f32),
            pltpu.SMEM((32,), jnp.int32),
            pltpu.VMEM((4, 2, 4, 128, 128), f32),
            pltpu.VMEM((4, 2, 4, 128, 128), f32),
            pltpu.VMEM((8, 512, 256), bf16),
            pltpu.VMEM((8, 512, 256), bf16),
            pltpu.VMEM((32, 128), f32),
            pltpu.VMEM((16, 128), f32),
            pltpu.VMEM((16, 8, 128), f32),
            pltpu.VMEM((NEWTON, ga, 1, 128), f32),
            pltpu.VMEM((NEWTON, gb, 1, 128), f32),
            pltpu.SemaphoreType.DMA((7,)),
            pltpu.SemaphoreType.DMA((SLOTS,)),
            pltpu.SemaphoreType.DMA((SLOTS,)),
            pltpu.SemaphoreType.DMA((SLOTS,)),
            pltpu.SemaphoreType.DMA((NEWTON,)),
            pltpu.SemaphoreType.DMA((NEWTON,)),
            pltpu.SemaphoreType.DMA((2 * NEWTON,)),
        ],
        compiler_params=pltpu.CompilerParams(
            collective_id=0, has_side_effects=True, vmem_limit_bytes=63 * 1024 * 1024
        ),
    )(state, explicit_blocks, implicit_blocks, pattern, cavity_mask, melt_rate, uptake_rate)
    return result.reshape(4, 2, 4, 128).transpose(2, 0, 1, 3)


def solution(mesh):
    nh, nd = mesh.shape["horiz"], mesh.shape["depth"]
    return jax.shard_map(
        functools.partial(per_device, nh, nd),
        mesh=mesh,
        in_specs=(
            P(None, "horiz", "depth", None),
            P("horiz", "depth", None, None, None),
            P("horiz", "depth", None, None, None),
            P("horiz", "depth", None),
            P("horiz", "depth", None),
            P("horiz", "depth", None),
            P("horiz", "depth", None),
        ),
        out_specs=P(None, "horiz", "depth", None),
        check_vma=False,
    )
```

```python
import functools
import jax
import jax.numpy as jnp
from jax import lax
from jax.experimental import pallas as pl
from jax.experimental.pallas import tpu as pltpu
from jax.sharding import PartitionSpec as P

NEWTON = 2
KRYLOV = 3
SHIFT = 0.3

f32 = jnp.float32
bf16 = jnp.bfloat16
MESH = pl.DeviceIdType.MESH

SLOT = 192
OWN = 80
CHANGED = 9
UPTAKE = 17
SLOTS = 18
ZERO = SLOTS * SLOT

DIRECTIONS = [(1, 1), (1, -1), (1, 0), (0, 1), (0, -1), (-1, 1), (-1, -1), (-1, 0)]


def rows(start, size):
    return pl.ds(pl.multiple_of(start, 16) if not isinstance(start, int) else start, size)


def kernel(
    nh, nd, ga, c_hbm, a_hbm, b_hbm, pat_hbm, mask_hbm, melt_hbm, upt_hbm, out,
    c_in, pat, mask, melt, upt, X, GB, IDX, st_a, st_b, WA, WB, FU, RA, RB,
    w_sem, r_sem, o_sem, s_sem, ra_sem, rb_sem, rs_sem, in_sem,
):
    gb = (nh // ga) * nd
    h = lax.axis_index("horiz")
    d = lax.axis_index("depth")

    h_hi = h // ga
    h_lo = lax.rem(h, ga)
    index_b = h_hi * nd + d

    sends = []
    outward = 2 * lax.rem(h, 2) - 1
    for side, sd in DIRECTIONS:
        n_rows = 16 if side else 32
        sh = side * outward
        src_h = 3 + sh if side else 2
        dst_h = 3 - 3 * sh if side else 2
        in_h = jnp.logical_and(h + sh >= 0, h + sh < nh)
        in_d = jnp.logical_and(d + sd >= 0, d + sd < nd)
        other_d = d + 1 - 2 * lax.rem(d, 2)
        other_h = h + 1 - 2 * lax.rem(h, 2)
        near_h = h + sh if side else other_h
        target = (
            jnp.where(in_h, jnp.where(in_d, h + sh, near_h), h),
            jnp.where(in_h, jnp.where(in_d, d + sd, d), other_d),
        )
        far_h = 3 + 3 * sh if side else 2
        position = jnp.where(
            in_h,
            jnp.where(in_d, (1 - sd) * 16 + dst_h * 2, (1 + sd) * 16 + dst_h * 2),
            (1 - sd) * 16 + far_h * 2,
        )
        sends.append((jnp.logical_and(in_h, in_d), (16 + src_h * 2) * 4, position * 4, n_rows, target, side == 1))

    nx = nh // ga
    far = lambda k, n: min(k, n - k)
    other_lo = h_lo + 1 - 2 * lax.rem(h_lo, 2)
    partners_a = [
        (h_hi * ga + lax.rem(h_lo + k, ga), d)
        for k in sorted(range(1, ga), key=lambda k: -far(k, ga))
    ]
    partners_b = [
        (lax.rem(h_hi + i, nx) * ga + other_lo, lax.rem(d + j, nd))
        for i, j in sorted(
            [(i, j) for i in range(nx) for j in range(nd) if i + j],
            key=lambda ij: -(far(ij[0], nx) + far(ij[1], nd)),
        )
    ]

    def ring(n, *offsets):
        return sorted({k % n for k in offsets} - {0})

    def along_z(*offsets):
        return [(h_hi * ga + lax.rem(h_lo + k, ga), d) for k in ring(ga, *offsets)]

    def along_x(*offsets):
        return [(lax.rem(h_hi + k, nx) * ga + h_lo, d) for k in ring(nx, *offsets)]

    def along_y(*offsets):
        return [(h, lax.rem(d + k, nd)) for k in ring(nd, *offsets)]

    nearest = along_z(1, -1) + along_x(1, -1) + along_y(1, -1)
    rounds = [
        nearest,
        along_z(2, -2) + along_x(1, -1, 2),
        along_z(4, -4) + [(h_hi * ga + other_lo, d)],
    ]

    def tell(number):
        for target in rounds[number]:
            pl.semaphore_signal(in_sem.at[number], inc=1, device_id=target, device_id_type=MESH)

    def told(number):
        pl.semaphore_wait(in_sem.at[number], len(rounds[number]))

    barrier = pltpu.get_barrier_semaphore()
    greeted = [target for *_, target, _ in sends] + nearest
    for target in greeted:
        pl.semaphore_signal(barrier, inc=1, device_id=target, device_id_type=MESH)

    small = [
        pltpu.make_async_copy(source, target, w_sem.at[2 + number])
        for number, (source, target) in enumerate(
            [(c_hbm, c_in), (upt_hbm, upt), (pat_hbm, pat), (mask_hbm, mask), (melt_hbm, melt)]
        )
    ]
    for copy in small:
        copy.start()
    copy_a = pltpu.make_async_copy(a_hbm, st_a, w_sem.at[0])
    copy_b = pltpu.make_async_copy(b_hbm, st_b, w_sem.at[1])
    copy_a.start()
    copy_b.start()

    for copy in small:
        copy.wait()
    for hh in range(4):
        for dd in range(2):
            o = hh * 2 + dd
            for t in range(4):
                X[pl.ds(OWN + o * 4 + t, 1), :] = c_in[t, hh, pl.ds(dd, 1), :]
            u_row = upt[hh, pl.ds(dd, 1), :]
            X[pl.ds(UPTAKE * SLOT + OWN + o * 4, 4), :] = jnp.broadcast_to(u_row, (4, 128))
            FU[pl.ds(o, 1), :] = mask[hh, pl.ds(dd, 1), :].astype(f32) * melt[hh, pl.ds(dd, 1), :]
            FU[pl.ds(8 + o, 1), :] = u_row
    X[pl.ds(ZERO, 32), :] = jnp.zeros((32, 128), f32)

    for o in range(8):
        for k in range(4):
            code = pat[o // 2, o % 2, k]
            five = lax.div(code, 5)
            row = (o // 2) + five
            dep = (o % 2) + code - 5 * five
            band = lax.div(dep, 2)
            IDX[o * 4 + k] = band * 16 + row * 2 + dep - 2 * band

    pl.semaphore_wait(barrier, len(greeted))

    def exchange(slot):
        base = slot * SLOT
        for inside, src, dst, n_rows, target, outer in sends:
            pltpu.make_async_remote_copy(
                src_ref=X.at[rows(jnp.where(inside, base + src, ZERO), n_rows)],
                dst_ref=X.at[rows(base + dst, n_rows)],
                send_sem=s_sem.at[slot],
                recv_sem=(o_sem if outer else r_sem).at[slot],
                device_id=target,
                device_id_type=MESH,
            ).start()

    def finished(slot, sem, size):
        span = X.at[rows(slot * SLOT, size)]
        pltpu.make_async_copy(span, span, sem.at[slot]).wait()

    def own(slot):
        return [X[pl.ds(slot * SLOT + OWN + t, 8, stride=4), :] for t in range(4)]

    def own_rows(slot):
        return X[rows(slot * SLOT + OWN, 32), :]

    def set_own(slot, value):
        for t in range(4):
            X[pl.ds(slot * SLOT + OWN + t, 8, stride=4), :] = value[t]

    def split_blocks(stage, weights):
        def body(o, _):
            for k in range(4):
                block = stage[o // 2, lax.rem(o, 2), k].T
                high = block.astype(bf16)
                weights[o, pl.ds(k * 128, 128), pl.ds(0, 128)] = high
                weights[o, pl.ds(k * 128, 128), pl.ds(128, 128)] = (block - high.astype(f32)).astype(bf16)
            return 0

        lax.fori_loop(0, 8, body, 0)

    upper = lax.broadcasted_iota(jnp.int32, (8, 128), 0) < 4

    core = lax.rem(h, 2)
    inner_rows = (1 - core) * 16
    outer_rows = core * 48

    def spread(slot, first, tiles):
        for band in range(3):
            for i in range(tiles):
                row = band * 64 + first + i * 8
                x = X[pl.ds(pl.multiple_of(slot * SLOT + row, 8), 8), :]
                high = x.astype(bf16).astype(f32)
                low = pltpu.roll(x - high, 4, axis=0)
                place = lax.div(row, 4)
                GB[place] = jnp.where(upper, high, low)
                GB[place + 1] = jnp.where(upper, low, high)

    def half_product(weights, first, target, sign):
        for pair in range(2):
            sums = []
            for o in (first + 2 * pair, first + 2 * pair + 1):
                lhs = jnp.concatenate([GB[IDX[o * 4 + k]].astype(bf16) for k in range(4)], axis=1)
                both = lax.dot_general(
                    lhs, weights[o], (((1,), (0,)), ((), ())), preferred_element_type=f32
                )
                both = both[:, :128] + both[:, 128:]
                sums.append(both + pltpu.roll(both, 4, axis=0))
            image = jnp.where(upper, sums[0], sums[1])
            place = pl.ds(pl.multiple_of(target * SLOT + OWN + first * 4 + pair * 8, 8), 8)
            X[place, :] = X[place, :] + image if sign > 0 else X[place, :] - image

    def product(slot, weights, target, sign=1, remote=True):
        if remote:
            finished(slot, r_sem, 112)
        spread(slot, inner_rows, 6)
        half_product(weights, 4 * (1 - core), target, sign)
        if remote:
            finished(slot, o_sem, 48)
        spread(slot, outer_rows, 2)
        half_product(weights, 4 * core, target, sign)

    def all_sum(step, row):
        RA[step, h_lo] = row

        for target in partners_a:
            pltpu.make_async_remote_copy(
                src_ref=RA.at[step, h_lo], dst_ref=RA.at[step, h_lo],
                send_sem=rs_sem.at[2 * step], recv_sem=ra_sem.at[step],
                device_id=target, device_id_type=MESH,
            ).start()
        span = RA.at[step, pl.ds(0, ga - 1)]
        pltpu.make_async_copy(span, span, ra_sem.at[step]).wait()
        RB[step, index_b] = jnp.sum(RA[step], axis=0)

        for target in partners_b:
            pltpu.make_async_remote_copy(
                src_ref=RB.at[step, index_b], dst_ref=RB.at[step, index_b],
                send_sem=rs_sem.at[2 * step + 1], recv_sem=rb_sem.at[step],
                device_id=target, device_id_type=MESH,
            ).start()
        span = RB.at[step, pl.ds(0, gb - 1)]
        pltpu.make_async_copy(span, span, rb_sem.at[step]).wait()
        return jnp.sum(RB[step], axis=0)

    lane = lax.broadcasted_iota(jnp.int32, (1, 128), 1)

    def coefficients(step, first):
        vectors = [[X[pl.ds((first + 2 * j) * SLOT + OWN + 8 * t, 8), :] for t in range(4)] for j in range(4)]
        pairs = [(i, j) for i in range(4) for j in range(i, 4)]
        row = jnp.zeros((1, 128), f32)
        for number, (i, j) in enumerate(pairs):
            part = sum(vectors[i][t] * vectors[j][t] for t in range(4))
            total = jnp.sum(jnp.sum(part, axis=0, keepdims=True), axis=1, keepdims=True)
            row = jnp.where(lane == number, total, row)
        total = all_sum(step, row)
        gram = {
            pair: jnp.sum(jnp.where(lane == number, total, 0.0), axis=1, keepdims=True)
            for number, pair in enumerate(pairs)
        }
        zero = jnp.zeros((1, 1), f32)
        R = [[zero] * 4 for _ in range(4)]
        for i in range(4):
            pivot = gram[i, i]
            for m in range(i):
                pivot = pivot - R[m][i] * R[m][i]
            pivot = jnp.maximum(pivot, 1e-14 * gram[i, i])
            R[i][i] = jnp.sqrt(pivot)
            inverse = 1.0 / R[i][i]
            for j in range(i + 1, 4):
                value = gram[i, j]
                for m in range(i):
                    value = value - R[m][i] * R[m][j]
                R[i][j] = value * inverse
        hess = [[(SHIFT - 1.0) * R[i][j] + R[i][j + 1] for j in range(3)] for i in range(4)]
        target = [R[0][0], zero, zero, zero]
        for c in range(3):
            top, low = hess[c][c], hess[c + 1][c]
            inverse = 1.0 / jnp.sqrt(top * top + low * low)
            cosine, sine = top * inverse, low * inverse
            for j in range(c, 3):
                top, low = hess[c][j], hess[c + 1][j]
                hess[c][j] = cosine * top + sine * low
                hess[c + 1][j] = cosine * low - sine * top
            top, low = target[c], target[c + 1]
            target[c] = cosine * top + sine * low
            target[c + 1] = cosine * low - sine * top
        answer = [zero] * 3
        for c in (2, 1, 0):
            value = target[c]
            for j in range(c + 1, 3):
                value = value - hess[c][j] * answer[j]
            answer[c] = value / hess[c][c]
        return answer

    def limitation(iron):
        squared = iron * iron
        return squared / (1.0 + squared)

    def slope(iron):
        denominator = 1.0 + iron * iron
        return 2.0 * iron / (denominator * denominator)

    def krylov(first, c):
        forcing, uptake = FU[pl.ds(0, 8), :], FU[pl.ds(8, 8), :]
        flux_one = uptake * limitation(c[3])
        flux_three = uptake * c[1] * slope(c[3])

        def step(j, _):
            slot = first + 2 * j
            exchange(slot)
            v = own(slot)
            change = flux_one * v[1] + flux_three * v[3]
            set_own(
                slot + 1,
                [
                    0.5 * v[0] - 0.5 * forcing * v[0],
                    0.5 * v[1] - 0.5 * change,
                    0.4 * v[2] + 0.25 * change,
                    0.5 * v[3] + 0.5 * forcing * v[0] - 0.025 * change,
                ],
            )
            product(slot, WA, slot + 1)
            exchange(slot + 1)
            X[rows((slot + 2) * SLOT + OWN, 32), :] = own_rows(slot + 1) - SHIFT * own_rows(slot)
            product(slot + 1, WB, slot + 2)
            return 0

        lax.fori_loop(0, KRYLOV, step, 0)

    exchange(0)
    tell(0)
    copy_a.wait()
    split_blocks(st_a, WA)
    c = own(0)
    forcing, uptake = FU[pl.ds(0, 8), :], FU[pl.ds(8, 8), :]
    flux = uptake * c[1] * limitation(c[3])
    source = [
        forcing * (1.0 - c[0]),
        -flux,
        0.5 * flux - 0.2 * c[2],
        forcing * c[0] - 0.05 * flux,
    ]
    set_own(1, [0.5 * c[t] + 0.5 * source[t] for t in range(4)])
    product(0, WA, 1)
    exchange(1)
    exchange(UPTAKE)
    copy_b.wait()
    split_blocks(st_b, WB)
    told(0)
    tell(1)
    X[rows(2 * SLOT + OWN, 32), :] = own_rows(0) - own_rows(1)
    product(1, WB, 2, sign=-1)
    told(1)
    tell(2)
    krylov(2, c)
    told(2)
    weights = coefficients(0, 2)

    finished(UPTAKE, r_sem, 112)
    finished(UPTAKE, o_sem, 48)

    def wide(slot, t):
        return X[pl.ds(slot * SLOT + t, 48, stride=4), :]

    def wide_sum(first_slot, t):
        return sum(weights[j] * wide(first_slot + 2 * j, t) for j in range(3))

    tracer_old, iron_old = wide(0, 1), wide(0, 3)
    iron_step = wide_sum(2, 3)
    tracer_new, iron_new = tracer_old + wide_sum(2, 1), iron_old + iron_step
    rest = wide(UPTAKE, 0) * (
        tracer_new * (limitation(iron_new) - limitation(iron_old)) - tracer_old * slope(iron_old) * iron_step
    )
    for t in range(4):
        value = wide(1, t) + wide_sum(3, t)
        if t:
            value = value + (0.0, -0.5, 0.25, -0.025)[t] * rest
        X[pl.ds(CHANGED * SLOT + t, 48, stride=4), :] = value
    changed = own_rows(0) + sum(weights[j] * own_rows(2 + 2 * j) for j in range(3))
    X[rows(10 * SLOT + OWN, 32), :] = changed - own_rows(CHANGED)
    product(CHANGED, WB, 10, sign=-1, remote=False)

    krylov(10, [own(0)[t] + sum(weights[j] * own(2 + 2 * j)[t] for j in range(3)) for t in range(4)])
    weights = coefficients(1, 10)
    out[...] = changed + sum(weights[j] * own_rows(10 + 2 * j) for j in range(3))

    for slot in (0, 1, 2, 3, 4, 5, 6, 7, 10, 11, 12, 13, 14, 15, UPTAKE):
        finished(slot, s_sem, 160)
    for step in range(NEWTON):
        span = RA.at[step, pl.ds(0, ga - 1)]
        pltpu.make_async_copy(span, span, rs_sem.at[2 * step]).wait()
        span = RB.at[step, pl.ds(0, gb - 1)]
        pltpu.make_async_copy(span, span, rs_sem.at[2 * step + 1]).wait()


def per_device(nh, nd, state, explicit_blocks, implicit_blocks, pattern, cavity_mask, melt_rate, uptake_rate):
    ga = 16 if nh % 16 == 0 else 2
    gb = (nh // ga) * nd
    vmem = pl.BlockSpec(memory_space=pltpu.VMEM)
    result = pl.pallas_call(
        functools.partial(kernel, nh, nd, ga),
        out_shape=jax.ShapeDtypeStruct((32, 128), f32),
        in_specs=[pl.BlockSpec(memory_space=pltpu.HBM)] * 7,
        out_specs=vmem,
        scratch_shapes=[
            pltpu.VMEM((4, 4, 2, 128), f32),
            pltpu.SMEM((4, 2, 4), jnp.int32),
            pltpu.VMEM((4, 2, 128), jnp.int32),
            pltpu.VMEM((4, 2, 128), f32),
            pltpu.VMEM((4, 2, 128), f32),
            pltpu.VMEM((SLOTS * SLOT + 32, 128), f32),
            pltpu.VMEM((48, 8, 128), f32),
            pltpu.SMEM((32,), jnp.int32),
            pltpu.VMEM((4, 2, 4, 128, 128), f32),
            pltpu.VMEM((4, 2, 4, 128, 128), f32),
            pltpu.VMEM((8, 512, 256), bf16),
            pltpu.VMEM((8, 512, 256), bf16),
            pltpu.VMEM((16, 128), f32),
            pltpu.VMEM((NEWTON, ga, 1, 128), f32),
            pltpu.VMEM((NEWTON, gb, 1, 128), f32),
            pltpu.SemaphoreType.DMA((7,)),
            pltpu.SemaphoreType.DMA((SLOTS,)),
            pltpu.SemaphoreType.DMA((SLOTS,)),
            pltpu.SemaphoreType.DMA((SLOTS,)),
            pltpu.SemaphoreType.DMA((NEWTON,)),
            pltpu.SemaphoreType.DMA((NEWTON,)),
            pltpu.SemaphoreType.DMA((2 * NEWTON,)),
            pltpu.SemaphoreType.REGULAR((3,)),
        ],
        compiler_params=pltpu.CompilerParams(
            collective_id=0, has_side_effects=True, vmem_limit_bytes=63 * 1024 * 1024
        ),
    )(state, explicit_blocks, implicit_blocks, pattern, cavity_mask, melt_rate, uptake_rate)
    return result.reshape(4, 2, 4, 128).transpose(2, 0, 1, 3)


def solution(mesh):
    nh, nd = mesh.shape["horiz"], mesh.shape["depth"]
    return jax.shard_map(
        functools.partial(per_device, nh, nd),
        mesh=mesh,
        in_specs=(
            P(None, "horiz", "depth", None),
            P("horiz", "depth", None, None, None),
            P("horiz", "depth", None, None, None),
            P("horiz", "depth", None),
            P("horiz", "depth", None),
            P("horiz", "depth", None),
            P("horiz", "depth", None),
        ),
        out_specs=P(None, "horiz", "depth", None),
        check_vma=False,
    )
```

```python
import functools
import jax
import jax.numpy as jnp
from jax import lax
from jax.experimental import pallas as pl
from jax.experimental.pallas import tpu as pltpu
from jax.sharding import PartitionSpec as P

NEWTON = 2
KRYLOV = 3
SHIFT = 0.3
SCALE = 0.015625

f32 = jnp.float32
bf16 = jnp.bfloat16
MESH = pl.DeviceIdType.MESH

SLOT = 192
OWN = 80
CHANGED = 9
UPTAKE = 17
SLOTS = 18
ZERO = SLOTS * SLOT

DIRECTIONS = [(1, 1), (1, -1), (1, 0), (0, 1), (0, -1), (-1, 1), (-1, -1), (-1, 0)]


def rows(start, size):
    return pl.ds(pl.multiple_of(start, 16) if not isinstance(start, int) else start, size)


def kernel(
    nh, nd, ga, c_hbm, a_hbm, b_hbm, pat_hbm, mask_hbm, melt_hbm, upt_hbm, out,
    c_in, pat, mask, melt, upt, X, GB, IDX, st_a, st_b, WA, WB, FU, RA, RB,
    w_sem, r_sem, o_sem, s_sem, ra_sem, rb_sem, rs_sem, in_sem,
):
    gb = (nh // ga) * nd
    h = lax.axis_index("horiz")
    d = lax.axis_index("depth")

    h_hi = h // ga
    h_lo = lax.rem(h, ga)
    index_b = h_hi * nd + d

    sends = []
    outward = 2 * lax.rem(h, 2) - 1
    for side, sd in DIRECTIONS:
        n_rows = 16 if side else 32
        sh = side * outward
        src_h = 3 + sh if side else 2
        dst_h = 3 - 3 * sh if side else 2
        in_h = jnp.logical_and(h + sh >= 0, h + sh < nh)
        in_d = jnp.logical_and(d + sd >= 0, d + sd < nd)
        other_d = d + 1 - 2 * lax.rem(d, 2)
        other_h = h + 1 - 2 * lax.rem(h, 2)
        near_h = h + sh if side else other_h
        target = (
            jnp.where(in_h, jnp.where(in_d, h + sh, near_h), h),
            jnp.where(in_h, jnp.where(in_d, d + sd, d), other_d),
        )
        far_h = 3 + 3 * sh if side else 2
        position = jnp.where(
            in_h,
            jnp.where(in_d, (1 - sd) * 16 + dst_h * 2, (1 + sd) * 16 + dst_h * 2),
            (1 - sd) * 16 + far_h * 2,
        )
        sends.append((jnp.logical_and(in_h, in_d), (16 + src_h * 2) * 4, position * 4, n_rows, target, side == 1))

    nx = nh // ga
    far = lambda k, n: min(k, n - k)
    other_lo = h_lo + 1 - 2 * lax.rem(h_lo, 2)
    partners_a = [
        (h_hi * ga + lax.rem(h_lo + k, ga), d)
        for k in sorted(range(1, ga), key=lambda k: -far(k, ga))
    ]
    partners_b = [
        (lax.rem(h_hi + i, nx) * ga + other_lo, lax.rem(d + j, nd))
        for i, j in sorted(
            [(i, j) for i in range(nx) for j in range(nd) if i + j],
            key=lambda ij: -(far(ij[0], nx) + far(ij[1], nd)),
        )
    ]

    def ring(n, *offsets):
        return sorted({k % n for k in offsets} - {0})

    def along_z(*offsets):
        return [(h_hi * ga + lax.rem(h_lo + k, ga), d) for k in ring(ga, *offsets)]

    def along_x(*offsets):
        return [(lax.rem(h_hi + k, nx) * ga + h_lo, d) for k in ring(nx, *offsets)]

    def along_y(*offsets):
        return [(h, lax.rem(d + k, nd)) for k in ring(nd, *offsets)]

    nearest = along_z(1, -1) + along_x(1, -1) + along_y(1, -1)
    rounds = [
        nearest,
        along_z(2, -2) + along_x(1, -1, 2),
        along_z(4, -4) + [(h_hi * ga + other_lo, d)],
    ]

    def tell(number):
        for target in rounds[number]:
            pl.semaphore_signal(in_sem.at[number], inc=1, device_id=target, device_id_type=MESH)

    def told(number):
        pl.semaphore_wait(in_sem.at[number], len(rounds[number]))

    barrier = pltpu.get_barrier_semaphore()
    greeted = [target for *_, target, _ in sends] + nearest
    for target in greeted:
        pl.semaphore_signal(barrier, inc=1, device_id=target, device_id_type=MESH)

    small = [
        pltpu.make_async_copy(source, target, w_sem.at[2 + number])
        for number, (source, target) in enumerate(
            [(c_hbm, c_in), (upt_hbm, upt), (pat_hbm, pat), (mask_hbm, mask), (melt_hbm, melt)]
        )
    ]
    for copy in small:
        copy.start()
    copy_a = pltpu.make_async_copy(a_hbm, st_a, w_sem.at[0])
    copy_b = pltpu.make_async_copy(b_hbm, st_b, w_sem.at[1])
    copy_a.start()
    copy_b.start()

    for copy in small:
        copy.wait()
    for hh in range(4):
        for dd in range(2):
            o = hh * 2 + dd
            for t in range(4):
                X[pl.ds(OWN + o * 4 + t, 1), :] = c_in[t, hh, pl.ds(dd, 1), :]
            u_row = upt[hh, pl.ds(dd, 1), :]
            X[pl.ds(UPTAKE * SLOT + OWN + o * 4, 4), :] = jnp.broadcast_to(u_row, (4, 128))
            FU[pl.ds(o, 1), :] = mask[hh, pl.ds(dd, 1), :].astype(f32) * melt[hh, pl.ds(dd, 1), :]
            FU[pl.ds(8 + o, 1), :] = u_row
    X[pl.ds(ZERO, 32), :] = jnp.zeros((32, 128), f32)

    for o in range(8):
        for k in range(4):
            code = pat[o // 2, o % 2, k]
            five = lax.div(code, 5)
            row = (o // 2) + five
            dep = (o % 2) + code - 5 * five
            band = lax.div(dep, 2)
            IDX[o * 4 + k] = band * 16 + row * 2 + dep - 2 * band

    pl.semaphore_wait(barrier, len(greeted))

    def exchange(slot):
        base = slot * SLOT
        for inside, src, dst, n_rows, target, outer in sends:
            pltpu.make_async_remote_copy(
                src_ref=X.at[rows(jnp.where(inside, base + src, ZERO), n_rows)],
                dst_ref=X.at[rows(base + dst, n_rows)],
                send_sem=s_sem.at[slot],
                recv_sem=(o_sem if outer else r_sem).at[slot],
                device_id=target,
                device_id_type=MESH,
            ).start()

    def finished(slot, sem, size):
        span = X.at[rows(slot * SLOT, size)]
        pltpu.make_async_copy(span, span, sem.at[slot]).wait()

    def own(slot):
        return [X[pl.ds(slot * SLOT + OWN + t, 8, stride=4), :] for t in range(4)]

    def own_rows(slot):
        return X[rows(slot * SLOT + OWN, 32), :]

    def set_own(slot, value):
        for t in range(4):
            X[pl.ds(slot * SLOT + OWN + t, 8, stride=4), :] = value[t]

    def split_blocks(stage, weights):
        def body(o, _):
            for k in range(4):
                block = stage[o // 2, lax.rem(o, 2), k].T
                high = block.astype(bf16)
                weights[o, pl.ds(k * 128, 128), pl.ds(0, 128)] = high
                weights[o, pl.ds(k * 128, 128), pl.ds(128, 128)] = (block - high.astype(f32)).astype(bf16)
            return 0

        lax.fori_loop(0, 8, body, 0)

    upper = lax.broadcasted_iota(jnp.int32, (8, 128), 0) < 4

    core = lax.rem(h, 2)
    inner_rows = (1 - core) * 16
    outer_rows = core * 48

    def spread(slot, first, tiles):
        for band in range(3):
            for i in range(tiles):
                row = band * 64 + first + i * 8
                x = X[pl.ds(pl.multiple_of(slot * SLOT + row, 8), 8), :]
                high = x.astype(bf16).astype(f32)
                low = pltpu.roll(x - high, 4, axis=0)
                place = lax.div(row, 4)
                GB[place] = jnp.where(upper, high, low)
                GB[place + 1] = jnp.where(upper, low, high)

    def half_product(weights, first, target, sign):
        for pair in range(2):
            sums = []
            for o in (first + 2 * pair, first + 2 * pair + 1):
                lhs = jnp.concatenate([GB[IDX[o * 4 + k]].astype(bf16) for k in range(4)], axis=1)
                both = lax.dot_general(
                    lhs, weights[o], (((1,), (0,)), ((), ())), preferred_element_type=f32
                )
                both = both[:, :128] + both[:, 128:]
                sums.append(both + pltpu.roll(both, 4, axis=0))
            image = jnp.where(upper, sums[0], sums[1])
            place = pl.ds(pl.multiple_of(target * SLOT + OWN + first * 4 + pair * 8, 8), 8)
            X[place, :] = X[place, :] + image if sign == 1 else X[place, :] + sign * image

    def product(slot, weights, target, sign=1, remote=True):
        if remote:
            finished(slot, r_sem, 112)
        spread(slot, inner_rows, 6)
        half_product(weights, 4 * (1 - core), target, sign)
        if remote:
            finished(slot, o_sem, 48)
        spread(slot, outer_rows, 2)
        half_product(weights, 4 * core, target, sign)

    def all_sum(step, row):
        RA[step, h_lo] = row

        for target in partners_a:
            pltpu.make_async_remote_copy(
                src_ref=RA.at[step, h_lo], dst_ref=RA.at[step, h_lo],
                send_sem=rs_sem.at[2 * step], recv_sem=ra_sem.at[step],
                device_id=target, device_id_type=MESH,
            ).start()
        span = RA.at[step, pl.ds(0, ga - 1)]
        pltpu.make_async_copy(span, span, ra_sem.at[step]).wait()
        RB[step, index_b] = jnp.sum(RA[step], axis=0)

        for target in partners_b:
            pltpu.make_async_remote_copy(
                src_ref=RB.at[step, index_b], dst_ref=RB.at[step, index_b],
                send_sem=rs_sem.at[2 * step + 1], recv_sem=rb_sem.at[step],
                device_id=target, device_id_type=MESH,
            ).start()
        span = RB.at[step, pl.ds(0, gb - 1)]
        pltpu.make_async_copy(span, span, rb_sem.at[step]).wait()
        return jnp.sum(RB[step], axis=0)

    lane = lax.broadcasted_iota(jnp.int32, (1, 128), 1)

    def coefficients(step, first):
        vectors = [[X[pl.ds((first + 2 * j) * SLOT + OWN + 8 * t, 8), :] for t in range(4)] for j in range(4)]
        pairs = [(i, j) for i in range(4) for j in range(i, 4)]
        row = jnp.zeros((1, 128), f32)
        for number, (i, j) in enumerate(pairs):
            part = sum(vectors[i][t] * vectors[j][t] for t in range(4))
            total = jnp.sum(jnp.sum(part, axis=0, keepdims=True), axis=1, keepdims=True)
            row = jnp.where(lane == number, total, row)
        total = all_sum(step, row)
        gram = {
            pair: jnp.sum(jnp.where(lane == number, total, 0.0), axis=1, keepdims=True)
            for number, pair in enumerate(pairs)
        }
        zero = jnp.zeros((1, 1), f32)
        R = [[zero] * 4 for _ in range(4)]
        for i in range(4):
            pivot = gram[i, i]
            for m in range(i):
                pivot = pivot - R[m][i] * R[m][i]
            pivot = jnp.maximum(pivot, 1e-14 * gram[i, i])
            R[i][i] = jnp.sqrt(pivot)
            inverse = 1.0 / R[i][i]
            for j in range(i + 1, 4):
                value = gram[i, j]
                for m in range(i):
                    value = value - R[m][i] * R[m][j]
                R[i][j] = value * inverse
        hess = [[(SHIFT - 1.0) * R[i][j] + R[i][j + 1] / SCALE for j in range(3)] for i in range(4)]
        target = [R[0][0], zero, zero, zero]
        for c in range(3):
            top, low = hess[c][c], hess[c + 1][c]
            inverse = 1.0 / jnp.sqrt(top * top + low * low)
            cosine, sine = top * inverse, low * inverse
            for j in range(c, 3):
                top, low = hess[c][j], hess[c + 1][j]
                hess[c][j] = cosine * top + sine * low
                hess[c + 1][j] = cosine * low - sine * top
            top, low = target[c], target[c + 1]
            target[c] = cosine * top + sine * low
            target[c + 1] = cosine * low - sine * top
        answer = [zero] * 3
        for c in (2, 1, 0):
            value = target[c]
            for j in range(c + 1, 3):
                value = value - hess[c][j] * answer[j]
            answer[c] = value / hess[c][c]
        return answer

    def limitation(iron):
        squared = iron * iron
        return squared / (1.0 + squared)

    def slope(iron):
        denominator = 1.0 + iron * iron
        return 2.0 * iron / (denominator * denominator)

    def krylov(first, c):
        forcing, uptake = FU[pl.ds(0, 8), :], FU[pl.ds(8, 8), :]
        flux_one = uptake * limitation(c[3])
        flux_three = uptake * c[1] * slope(c[3])

        def step(j, _):
            slot = first + 2 * j
            exchange(slot)
            v = own(slot)
            change = flux_one * v[1] + flux_three * v[3]
            set_own(
                slot + 1,
                [
                    0.5 * v[0] - 0.5 * forcing * v[0],
                    0.5 * v[1] - 0.5 * change,
                    0.4 * v[2] + 0.25 * change,
                    0.5 * v[3] + 0.5 * forcing * v[0] - 0.025 * change,
                ],
            )
            product(slot, WA, slot + 1)
            exchange(slot + 1)
            X[rows((slot + 2) * SLOT + OWN, 32), :] = SCALE * (own_rows(slot + 1) - SHIFT * own_rows(slot))
            product(slot + 1, WB, slot + 2, sign=SCALE)
            return 0

        lax.fori_loop(0, KRYLOV, step, 0)

    exchange(0)
    tell(0)
    copy_a.wait()
    split_blocks(st_a, WA)
    c = own(0)
    forcing, uptake = FU[pl.ds(0, 8), :], FU[pl.ds(8, 8), :]
    flux = uptake * c[1] * limitation(c[3])
    source = [
        forcing * (1.0 - c[0]),
        -flux,
        0.5 * flux - 0.2 * c[2],
        forcing * c[0] - 0.05 * flux,
    ]
    set_own(1, [0.5 * c[t] + 0.5 * source[t] for t in range(4)])
    product(0, WA, 1)
    exchange(1)
    exchange(UPTAKE)
    copy_b.wait()
    split_blocks(st_b, WB)
    told(0)
    tell(1)
    X[rows(2 * SLOT + OWN, 32), :] = own_rows(0) - own_rows(1)
    product(1, WB, 2, sign=-1)
    told(1)
    tell(2)
    krylov(2, c)
    told(2)
    weights = coefficients(0, 2)

    finished(UPTAKE, r_sem, 112)
    finished(UPTAKE, o_sem, 48)

    def wide(slot, t):
        return X[pl.ds(slot * SLOT + t, 48, stride=4), :]

    def wide_sum(first_slot, t):
        return sum(weights[j] * wide(first_slot + 2 * j, t) for j in range(3))

    tracer_old, iron_old = wide(0, 1), wide(0, 3)
    iron_step = wide_sum(2, 3)
    tracer_new, iron_new = tracer_old + wide_sum(2, 1), iron_old + iron_step
    rest = wide(UPTAKE, 0) * (
        tracer_new * (limitation(iron_new) - limitation(iron_old)) - tracer_old * slope(iron_old) * iron_step
    )
    for t in range(4):
        value = wide(1, t) + wide_sum(3, t)
        if t:
            value = value + (0.0, -0.5, 0.25, -0.025)[t] * rest
        X[pl.ds(CHANGED * SLOT + t, 48, stride=4), :] = value
    changed = own_rows(0) + sum(weights[j] * own_rows(2 + 2 * j) for j in range(3))
    X[rows(10 * SLOT + OWN, 32), :] = changed - own_rows(CHANGED)
    product(CHANGED, WB, 10, sign=-1, remote=False)

    krylov(10, [own(0)[t] + sum(weights[j] * own(2 + 2 * j)[t] for j in range(3)) for t in range(4)])
    weights = coefficients(1, 10)
    out[...] = changed + sum(weights[j] * own_rows(10 + 2 * j) for j in range(3))

    for slot in (0, 1, 2, 3, 4, 5, 6, 7, 10, 11, 12, 13, 14, 15, UPTAKE):
        finished(slot, s_sem, 160)
    for step in range(NEWTON):
        span = RA.at[step, pl.ds(0, ga - 1)]
        pltpu.make_async_copy(span, span, rs_sem.at[2 * step]).wait()
        span = RB.at[step, pl.ds(0, gb - 1)]
        pltpu.make_async_copy(span, span, rs_sem.at[2 * step + 1]).wait()


def per_device(nh, nd, state, explicit_blocks, implicit_blocks, pattern, cavity_mask, melt_rate, uptake_rate):
    ga = 16 if nh % 16 == 0 else 2
    gb = (nh // ga) * nd
    vmem = pl.BlockSpec(memory_space=pltpu.VMEM)
    result = pl.pallas_call(
        functools.partial(kernel, nh, nd, ga),
        out_shape=jax.ShapeDtypeStruct((32, 128), f32),
        in_specs=[pl.BlockSpec(memory_space=pltpu.HBM)] * 7,
        out_specs=vmem,
        scratch_shapes=[
            pltpu.VMEM((4, 4, 2, 128), f32),
            pltpu.SMEM((4, 2, 4), jnp.int32),
            pltpu.VMEM((4, 2, 128), jnp.int32),
            pltpu.VMEM((4, 2, 128), f32),
            pltpu.VMEM((4, 2, 128), f32),
            pltpu.VMEM((SLOTS * SLOT + 32, 128), f32),
            pltpu.VMEM((48, 8, 128), f32),
            pltpu.SMEM((32,), jnp.int32),
            pltpu.VMEM((4, 2, 4, 128, 128), f32),
            pltpu.VMEM((4, 2, 4, 128, 128), f32),
            pltpu.VMEM((8, 512, 256), bf16),
            pltpu.VMEM((8, 512, 256), bf16),
            pltpu.VMEM((16, 128), f32),
            pltpu.VMEM((NEWTON, ga, 1, 128), f32),
            pltpu.VMEM((NEWTON, gb, 1, 128), f32),
            pltpu.SemaphoreType.DMA((7,)),
            pltpu.SemaphoreType.DMA((SLOTS,)),
            pltpu.SemaphoreType.DMA((SLOTS,)),
            pltpu.SemaphoreType.DMA((SLOTS,)),
            pltpu.SemaphoreType.DMA((NEWTON,)),
            pltpu.SemaphoreType.DMA((NEWTON,)),
            pltpu.SemaphoreType.DMA((2 * NEWTON,)),
            pltpu.SemaphoreType.REGULAR((3,)),
        ],
        compiler_params=pltpu.CompilerParams(
            collective_id=0, has_side_effects=True, vmem_limit_bytes=63 * 1024 * 1024
        ),
    )(state, explicit_blocks, implicit_blocks, pattern, cavity_mask, melt_rate, uptake_rate)
    return result.reshape(4, 2, 4, 128).transpose(2, 0, 1, 3)


def solution(mesh):
    nh, nd = mesh.shape["horiz"], mesh.shape["depth"]
    return jax.shard_map(
        functools.partial(per_device, nh, nd),
        mesh=mesh,
        in_specs=(
            P(None, "horiz", "depth", None),
            P("horiz", "depth", None, None, None),
            P("horiz", "depth", None, None, None),
            P("horiz", "depth", None),
            P("horiz", "depth", None),
            P("horiz", "depth", None),
            P("horiz", "depth", None),
        ),
        out_specs=P(None, "horiz", "depth", None),
        check_vma=False,
    )
```

```python
import functools
import jax
import jax.numpy as jnp
from jax import lax
from jax.experimental import pallas as pl
from jax.experimental.pallas import tpu as pltpu
from jax.sharding import PartitionSpec as P

NEWTON = 2
KRYLOV = 3
SHIFT = 0.3
SCALE = 0.015625

f32 = jnp.float32
bf16 = jnp.bfloat16
MESH = pl.DeviceIdType.MESH

SLOT = 192
OWN = 80
CHANGED = 9
UPTAKE = 17
SLOTS = 18
ZERO = SLOTS * SLOT

DIRECTIONS = [(1, 1), (1, -1), (1, 0), (0, 1), (0, -1), (-1, 1), (-1, -1), (-1, 0)]


def rows(start, size):
    return pl.ds(pl.multiple_of(start, 16) if not isinstance(start, int) else start, size)


def kernel(
    nh, nd, ga, c_hbm, a_hbm, b_hbm, pat_hbm, mask_hbm, melt_hbm, upt_hbm, out,
    c_in, pat, mask, melt, upt, X, GB, IDX, st_a, st_b, WA, WB, FU, RA, RB,
    w_sem, r_sem, o_sem, s_sem, ra_sem, rb_sem, rs_sem, in_sem,
):
    gb = (nh // ga) * nd
    h = lax.axis_index("horiz")
    d = lax.axis_index("depth")

    h_hi = h // ga
    h_lo = lax.rem(h, ga)
    index_b = h_hi * nd + d

    sends = []
    outward = 2 * lax.rem(h, 2) - 1
    for side, sd in DIRECTIONS:
        n_rows = 16 if side else 32
        sh = side * outward
        src_h = 3 + sh if side else 2
        dst_h = 3 - 3 * sh if side else 2
        in_h = jnp.logical_and(h + sh >= 0, h + sh < nh)
        in_d = jnp.logical_and(d + sd >= 0, d + sd < nd)
        other_d = d + 1 - 2 * lax.rem(d, 2)
        other_h = h + 1 - 2 * lax.rem(h, 2)
        near_h = h + sh if side else other_h
        target = (
            jnp.where(in_h, jnp.where(in_d, h + sh, near_h), h),
            jnp.where(in_h, jnp.where(in_d, d + sd, d), other_d),
        )
        far_h = 3 + 3 * sh if side else 2
        position = jnp.where(
            in_h,
            jnp.where(in_d, (1 - sd) * 16 + dst_h * 2, (1 + sd) * 16 + dst_h * 2),
            (1 - sd) * 16 + far_h * 2,
        )
        sends.append((jnp.logical_and(in_h, in_d), (16 + src_h * 2) * 4, position * 4, n_rows, target, side == 1))

    nx = nh // ga
    far = lambda k, n: min(k, n - k)
    other_lo = h_lo + 1 - 2 * lax.rem(h_lo, 2)
    core = lax.rem(h, 2)
    half = ga // 2
    z = lax.div(h_lo, 2)
    index_a = (h_hi * nd + d) * 2 + core
    partners_a = [
        (lax.rem(h_hi + i, nx) * ga + (other_lo if flip else h_lo), lax.rem(d + j, nd))
        for i, j, flip in sorted(
            [(i, j, f) for i in range(nx) for j in range(nd) for f in (0, 1) if i + j + f],
            key=lambda p: -(far(p[0], nx) + far(p[1], nd)) + 0.5 * p[2],
        )
    ]
    partners_b = [
        (h_hi * ga + lax.rem(z + k, half) * 2 + 1 - core, d)
        for k in sorted(range(1, half), key=lambda k: -far(k, half))
    ]

    def ring(n, *offsets):
        return sorted({k % n for k in offsets} - {0})

    def along_z(*offsets):
        return [(h_hi * ga + lax.rem(h_lo + k, ga), d) for k in ring(ga, *offsets)]

    def along_x(*offsets):
        return [(lax.rem(h_hi + k, nx) * ga + h_lo, d) for k in ring(nx, *offsets)]

    def along_y(*offsets):
        return [(h, lax.rem(d + k, nd)) for k in ring(nd, *offsets)]

    nearest = along_z(1, -1) + along_x(1, -1) + along_y(1, -1)
    rounds = [
        nearest,
        along_z(2, -2) + along_x(1, -1, 2),
        along_z(4, -4) + [(h_hi * ga + other_lo, d)],
    ]

    def tell(number):
        for target in rounds[number]:
            pl.semaphore_signal(in_sem.at[number], inc=1, device_id=target, device_id_type=MESH)

    def told(number):
        pl.semaphore_wait(in_sem.at[number], len(rounds[number]))

    barrier = pltpu.get_barrier_semaphore()
    greeted = [target for *_, target, _ in sends] + nearest
    for target in greeted:
        pl.semaphore_signal(barrier, inc=1, device_id=target, device_id_type=MESH)

    small = [
        pltpu.make_async_copy(source, target, w_sem.at[2 + number])
        for number, (source, target) in enumerate(
            [(c_hbm, c_in), (upt_hbm, upt), (pat_hbm, pat), (mask_hbm, mask), (melt_hbm, melt)]
        )
    ]
    for copy in small:
        copy.start()
    copy_a = pltpu.make_async_copy(a_hbm, st_a, w_sem.at[0])
    copy_b = pltpu.make_async_copy(b_hbm, st_b, w_sem.at[1])
    copy_a.start()
    copy_b.start()

    for copy in small:
        copy.wait()
    for hh in range(4):
        for dd in range(2):
            o = hh * 2 + dd
            for t in range(4):
                X[pl.ds(OWN + o * 4 + t, 1), :] = c_in[t, hh, pl.ds(dd, 1), :]
            u_row = upt[hh, pl.ds(dd, 1), :]
            X[pl.ds(UPTAKE * SLOT + OWN + o * 4, 4), :] = jnp.broadcast_to(u_row, (4, 128))
            FU[pl.ds(o, 1), :] = mask[hh, pl.ds(dd, 1), :].astype(f32) * melt[hh, pl.ds(dd, 1), :]
            FU[pl.ds(8 + o, 1), :] = u_row
    X[pl.ds(ZERO, 32), :] = jnp.zeros((32, 128), f32)

    for o in range(8):
        for k in range(4):
            code = pat[o // 2, o % 2, k]
            five = lax.div(code, 5)
            row = (o // 2) + five
            dep = (o % 2) + code - 5 * five
            band = lax.div(dep, 2)
            IDX[o * 4 + k] = band * 16 + row * 2 + dep - 2 * band

    pl.semaphore_wait(barrier, len(greeted))

    def exchange(slot):
        base = slot * SLOT
        for inside, src, dst, n_rows, target, outer in sends:
            pltpu.make_async_remote_copy(
                src_ref=X.at[rows(jnp.where(inside, base + src, ZERO), n_rows)],
                dst_ref=X.at[rows(base + dst, n_rows)],
                send_sem=s_sem.at[slot],
                recv_sem=(o_sem if outer else r_sem).at[slot],
                device_id=target,
                device_id_type=MESH,
            ).start()

    def finished(slot, sem, size):
        span = X.at[rows(slot * SLOT, size)]
        pltpu.make_async_copy(span, span, sem.at[slot]).wait()

    def own(slot):
        return [X[pl.ds(slot * SLOT + OWN + t, 8, stride=4), :] for t in range(4)]

    def own_rows(slot):
        return X[rows(slot * SLOT + OWN, 32), :]

    def set_own(slot, value):
        for t in range(4):
            X[pl.ds(slot * SLOT + OWN + t, 8, stride=4), :] = value[t]

    def split_blocks(stage, weights):
        def body(o, _):
            for k in range(4):
                block = stage[o // 2, lax.rem(o, 2), k].T
                high = block.astype(bf16)
                weights[o, pl.ds(k * 128, 128), pl.ds(0, 128)] = high
                weights[o, pl.ds(k * 128, 128), pl.ds(128, 128)] = (block - high.astype(f32)).astype(bf16)
            return 0

        lax.fori_loop(0, 8, body, 0)

    upper = lax.broadcasted_iota(jnp.int32, (8, 128), 0) < 4

    inner_rows = (1 - core) * 16
    outer_rows = core * 48

    def spread(slot, first, tiles):
        for band in range(3):
            for i in range(tiles):
                row = band * 64 + first + i * 8
                x = X[pl.ds(pl.multiple_of(slot * SLOT + row, 8), 8), :]
                high = x.astype(bf16).astype(f32)
                low = pltpu.roll(x - high, 4, axis=0)
                place = lax.div(row, 4)
                GB[place] = jnp.where(upper, high, low)
                GB[place + 1] = jnp.where(upper, low, high)

    def half_product(weights, first, target, sign):
        for pair in range(2):
            sums = []
            for o in (first + 2 * pair, first + 2 * pair + 1):
                lhs = jnp.concatenate([GB[IDX[o * 4 + k]].astype(bf16) for k in range(4)], axis=1)
                both = lax.dot_general(
                    lhs, weights[o], (((1,), (0,)), ((), ())), preferred_element_type=f32
                )
                both = both[:, :128] + both[:, 128:]
                sums.append(both + pltpu.roll(both, 4, axis=0))
            image = jnp.where(upper, sums[0], sums[1])
            place = pl.ds(pl.multiple_of(target * SLOT + OWN + first * 4 + pair * 8, 8), 8)
            X[place, :] = X[place, :] + image if sign == 1 else X[place, :] + sign * image

    def product(slot, weights, target, sign=1, remote=True):
        if remote:
            finished(slot, r_sem, 112)
        spread(slot, inner_rows, 6)
        half_product(weights, 4 * (1 - core), target, sign)
        if remote:
            finished(slot, o_sem, 48)
        spread(slot, outer_rows, 2)
        half_product(weights, 4 * core, target, sign)

    def all_sum(step, row):
        RA[step, index_a] = row

        for target in partners_a:
            pltpu.make_async_remote_copy(
                src_ref=RA.at[step, index_a], dst_ref=RA.at[step, index_a],
                send_sem=rs_sem.at[2 * step], recv_sem=ra_sem.at[step],
                device_id=target, device_id_type=MESH,
            ).start()
        span = RA.at[step, pl.ds(0, 2 * gb - 1)]
        pltpu.make_async_copy(span, span, ra_sem.at[step]).wait()
        RB[step, z] = jnp.sum(RA[step], axis=0)

        for target in partners_b:
            pltpu.make_async_remote_copy(
                src_ref=RB.at[step, z], dst_ref=RB.at[step, z],
                send_sem=rs_sem.at[2 * step + 1], recv_sem=rb_sem.at[step],
                device_id=target, device_id_type=MESH,
            ).start()
        span = RB.at[step, pl.ds(0, half - 1)]
        pltpu.make_async_copy(span, span, rb_sem.at[step]).wait()
        return jnp.sum(RB[step], axis=0)

    lane = lax.broadcasted_iota(jnp.int32, (1, 128), 1)

    def coefficients(step, first):
        vectors = [[X[pl.ds((first + 2 * j) * SLOT + OWN + 8 * t, 8), :] for t in range(4)] for j in range(4)]
        pairs = [(i, j) for i in range(4) for j in range(i, 4)]
        row = jnp.zeros((1, 128), f32)
        for number, (i, j) in enumerate(pairs):
            part = sum(vectors[i][t] * vectors[j][t] for t in range(4))
            total = jnp.sum(jnp.sum(part, axis=0, keepdims=True), axis=1, keepdims=True)
            row = jnp.where(lane == number, total, row)
        total = all_sum(step, row)
        gram = {
            pair: jnp.sum(jnp.where(lane == number, total, 0.0), axis=1, keepdims=True)
            for number, pair in enumerate(pairs)
        }
        zero = jnp.zeros((1, 1), f32)
        R = [[zero] * 4 for _ in range(4)]
        for i in range(4):
            pivot = gram[i, i]
            for m in range(i):
                pivot = pivot - R[m][i] * R[m][i]
            pivot = jnp.maximum(pivot, 1e-14 * gram[i, i])
            R[i][i] = jnp.sqrt(pivot)
            inverse = 1.0 / R[i][i]
            for j in range(i + 1, 4):
                value = gram[i, j]
                for m in range(i):
                    value = value - R[m][i] * R[m][j]
                R[i][j] = value * inverse
        hess = [[(SHIFT - 1.0) * R[i][j] + R[i][j + 1] / SCALE for j in range(3)] for i in range(4)]
        target = [R[0][0], zero, zero, zero]
        for c in range(3):
            top, low = hess[c][c], hess[c + 1][c]
            inverse = 1.0 / jnp.sqrt(top * top + low * low)
            cosine, sine = top * inverse, low * inverse
            for j in range(c, 3):
                top, low = hess[c][j], hess[c + 1][j]
                hess[c][j] = cosine * top + sine * low
                hess[c + 1][j] = cosine * low - sine * top
            top, low = target[c], target[c + 1]
            target[c] = cosine * top + sine * low
            target[c + 1] = cosine * low - sine * top
        answer = [zero] * 3
        for c in (2, 1, 0):
            value = target[c]
            for j in range(c + 1, 3):
                value = value - hess[c][j] * answer[j]
            answer[c] = value / hess[c][c]
        return answer

    def limitation(iron):
        squared = iron * iron
        return squared / (1.0 + squared)

    def slope(iron):
        denominator = 1.0 + iron * iron
        return 2.0 * iron / (denominator * denominator)

    def krylov(first, c):
        forcing, uptake = FU[pl.ds(0, 8), :], FU[pl.ds(8, 8), :]
        flux_one = uptake * limitation(c[3])
        flux_three = uptake * c[1] * slope(c[3])

        def step(j, _):
            slot = first + 2 * j
            exchange(slot)
            v = own(slot)
            change = flux_one * v[1] + flux_three * v[3]
            set_own(
                slot + 1,
                [
                    0.5 * v[0] - 0.5 * forcing * v[0],
                    0.5 * v[1] - 0.5 * change,
                    0.4 * v[2] + 0.25 * change,
                    0.5 * v[3] + 0.5 * forcing * v[0] - 0.025 * change,
                ],
            )
            product(slot, WA, slot + 1)
            exchange(slot + 1)
            X[rows((slot + 2) * SLOT + OWN, 32), :] = SCALE * (own_rows(slot + 1) - SHIFT * own_rows(slot))
            product(slot + 1, WB, slot + 2, sign=SCALE)
            return 0

        lax.fori_loop(0, KRYLOV, step, 0)

    exchange(0)
    tell(0)
    copy_a.wait()
    split_blocks(st_a, WA)
    c = own(0)
    forcing, uptake = FU[pl.ds(0, 8), :], FU[pl.ds(8, 8), :]
    flux = uptake * c[1] * limitation(c[3])
    source = [
        forcing * (1.0 - c[0]),
        -flux,
        0.5 * flux - 0.2 * c[2],
        forcing * c[0] - 0.05 * flux,
    ]
    set_own(1, [0.5 * c[t] + 0.5 * source[t] for t in range(4)])
    product(0, WA, 1)
    exchange(1)
    exchange(UPTAKE)
    copy_b.wait()
    split_blocks(st_b, WB)
    told(0)
    tell(1)
    X[rows(2 * SLOT + OWN, 32), :] = own_rows(0) - own_rows(1)
    product(1, WB, 2, sign=-1)
    told(1)
    tell(2)
    krylov(2, c)
    told(2)
    weights = coefficients(0, 2)

    finished(UPTAKE, r_sem, 112)
    finished(UPTAKE, o_sem, 48)

    def wide(slot, t):
        return X[pl.ds(slot * SLOT + t, 48, stride=4), :]

    def wide_sum(first_slot, t):
        return sum(weights[j] * wide(first_slot + 2 * j, t) for j in range(3))

    tracer_old, iron_old = wide(0, 1), wide(0, 3)
    iron_step = wide_sum(2, 3)
    tracer_new, iron_new = tracer_old + wide_sum(2, 1), iron_old + iron_step
    rest = wide(UPTAKE, 0) * (
        tracer_new * (limitation(iron_new) - limitation(iron_old)) - tracer_old * slope(iron_old) * iron_step
    )
    for t in range(4):
        value = wide(1, t) + wide_sum(3, t)
        if t:
            value = value + (0.0, -0.5, 0.25, -0.025)[t] * rest
        X[pl.ds(CHANGED * SLOT + t, 48, stride=4), :] = value
    changed = own_rows(0) + sum(weights[j] * own_rows(2 + 2 * j) for j in range(3))
    X[rows(10 * SLOT + OWN, 32), :] = changed - own_rows(CHANGED)
    product(CHANGED, WB, 10, sign=-1, remote=False)

    krylov(10, [own(0)[t] + sum(weights[j] * own(2 + 2 * j)[t] for j in range(3)) for t in range(4)])
    weights = coefficients(1, 10)
    out[...] = changed + sum(weights[j] * own_rows(10 + 2 * j) for j in range(3))

    for slot in (0, 1, 2, 3, 4, 5, 6, 7, 10, 11, 12, 13, 14, 15, UPTAKE):
        finished(slot, s_sem, 160)
    for step in range(NEWTON):
        span = RA.at[step, pl.ds(0, 2 * gb - 1)]
        pltpu.make_async_copy(span, span, rs_sem.at[2 * step]).wait()
        span = RB.at[step, pl.ds(0, half - 1)]
        pltpu.make_async_copy(span, span, rs_sem.at[2 * step + 1]).wait()


def per_device(nh, nd, state, explicit_blocks, implicit_blocks, pattern, cavity_mask, melt_rate, uptake_rate):
    ga = 16 if nh % 16 == 0 else 2
    gb = (nh // ga) * nd
    vmem = pl.BlockSpec(memory_space=pltpu.VMEM)
    result = pl.pallas_call(
        functools.partial(kernel, nh, nd, ga),
        out_shape=jax.ShapeDtypeStruct((32, 128), f32),
        in_specs=[pl.BlockSpec(memory_space=pltpu.HBM)] * 7,
        out_specs=vmem,
        scratch_shapes=[
            pltpu.VMEM((4, 4, 2, 128), f32),
            pltpu.SMEM((4, 2, 4), jnp.int32),
            pltpu.VMEM((4, 2, 128), jnp.int32),
            pltpu.VMEM((4, 2, 128), f32),
            pltpu.VMEM((4, 2, 128), f32),
            pltpu.VMEM((SLOTS * SLOT + 32, 128), f32),
            pltpu.VMEM((48, 8, 128), f32),
            pltpu.SMEM((32,), jnp.int32),
            pltpu.VMEM((4, 2, 4, 128, 128), f32),
            pltpu.VMEM((4, 2, 4, 128, 128), f32),
            pltpu.VMEM((8, 512, 256), bf16),
            pltpu.VMEM((8, 512, 256), bf16),
            pltpu.VMEM((16, 128), f32),
            pltpu.VMEM((NEWTON, 2 * gb, 1, 128), f32),
            pltpu.VMEM((NEWTON, ga // 2, 1, 128), f32),
            pltpu.SemaphoreType.DMA((7,)),
            pltpu.SemaphoreType.DMA((SLOTS,)),
            pltpu.SemaphoreType.DMA((SLOTS,)),
            pltpu.SemaphoreType.DMA((SLOTS,)),
            pltpu.SemaphoreType.DMA((NEWTON,)),
            pltpu.SemaphoreType.DMA((NEWTON,)),
            pltpu.SemaphoreType.DMA((2 * NEWTON,)),
            pltpu.SemaphoreType.REGULAR((3,)),
        ],
        compiler_params=pltpu.CompilerParams(
            collective_id=0, has_side_effects=True, vmem_limit_bytes=63 * 1024 * 1024
        ),
    )(state, explicit_blocks, implicit_blocks, pattern, cavity_mask, melt_rate, uptake_rate)
    return result.reshape(4, 2, 4, 128).transpose(2, 0, 1, 3)


def solution(mesh):
    nh, nd = mesh.shape["horiz"], mesh.shape["depth"]
    return jax.shard_map(
        functools.partial(per_device, nh, nd),
        mesh=mesh,
        in_specs=(
            P(None, "horiz", "depth", None),
            P("horiz", "depth", None, None, None),
            P("horiz", "depth", None, None, None),
            P("horiz", "depth", None),
            P("horiz", "depth", None),
            P("horiz", "depth", None),
            P("horiz", "depth", None),
        ),
        out_specs=P(None, "horiz", "depth", None),
        check_vma=False,
    )
```
